128 devices in a mesh: dp: 8 (over z_hi, y), seq: 16 (over z_lo, x, core).
Axes of the slice: x: 4, y: 4, z: 4 (z_hi: 2, z_lo: 2; z = z_hi * 2 + z_lo), core: 2. Of those that a mesh axis runs over, the one named last changes fastest.
Arguments:
- qkv_txt: bfloat16 [8, 512, 6144], P('dp', 'seq'), may hold values from -6 to 6
- qkv_img: bfloat16 [8, 2048, 6144], P('dp', 'seq'), may hold values from -8 to 8
- attn_img: bfloat16 [8, 2048, 2048], P('dp', 'seq'), may hold values from -6 to 6
- cot_txt: bfloat16 [8, 512, 2048], P('dp', 'seq'), may hold values from -320 to 320
- cot_img: bfloat16 [8, 2048, 3072], P('dp', 'seq'), may hold values from -320 to 320
- gate: float32 [8, 3072], P('dp'), may hold values from 0.1 to 1.9
- advantage: float32 [8], P('dp'), may hold values from -3 to 3
- proj_weight: bfloat16 [2048, 3072], replicated, may hold values from -0.125 to 0.125
Outputs:
- dqkv_txt: bfloat16 [8, 512, 6144], P('dp', 'seq')
- dqkv_img: bfloat16 [8, 2048, 6144], P('dp', 'seq')
- grad_proj: float32 [2048, 3072], P(('dp', 'seq'))
The draws below stay inside these ranges and needn't reach their ends.
All inputs are finite; a program needn't handle non-finite values.
Results may differ from the reference program's by a relative error of at most 0.0077.
Values may be sent and summed in bfloat16 or wider, within the bound.
No kernel may reach another device: no remote copies, remote signals or barrier semaphores. Data moves between devices by JAX's collectives and lax.ppermute only.
A program may use at most 192 MiB of HBM per device.

```python
import jax
import jax.numpy as jnp
from jax import lax

D = 3072
HEADS = 16
HEAD_SIZE = 128
HD = 2048
BATCH = 8
IMG = 2048
TXT = 512
JOINT = 2560


def draw_qkv_img(key, part):
    key = jax.random.fold_in(key, 11)
    shape = (BATCH, IMG, 3 * HD)
    values = jnp.clip(jax.random.normal(key, shape, jnp.float32), -8.0, 8.0)
    return values.astype(jnp.bfloat16)


def spiked(drawn, own_key, source, target, parts, factor):
    owner, partner = [(jnp.arange(drawn.shape[dim]) // (drawn.shape[dim] // parts)).reshape([-1 if axis == dim else 1 for axis in range(drawn.ndim)]) for dim in (source, target)]
    chosen = jax.random.permutation(own_key, parts)[partner]
    strong = (owner == chosen) | (owner == (partner + parts // 2) % parts)
    return jnp.where(strong, factor * drawn, drawn)


def block_scale(own_key, shape, split, least, high):
    factor_of = 1.0
    for position, blocks in split:
        steps = jax.random.uniform(jax.random.fold_in(jax.random.fold_in(own_key, 6), position), (blocks,), jnp.float32, least / len(split), high / len(split))
        factor_of = factor_of * jnp.repeat(jnp.exp(steps), shape[position] // blocks).reshape((-1,) + (1,) * (len(shape) - 1 - position))
    return factor_of


def noise(stream_key, dims, width, most, cuts=(), dtype=jnp.bfloat16):
    drawn = width * jax.random.normal(stream_key, dims, jnp.float32)
    if cuts:
        drawn = drawn * block_scale(stream_key, dims, cuts, -0.22, 0.18)
    return jnp.clip(drawn, -most, most).astype(dtype)


def noise_with(own_key, extent, deviation, bound, shards, heavy, kind=jnp.bfloat16):
    values = deviation * jax.random.normal(own_key, extent, jnp.float32)
    if shards:
        values = values * block_scale(own_key, extent, shards, -0.22, 0.18)
    return jnp.clip(spiked(values, jax.random.fold_in(own_key, 3), *heavy), -bound, bound).astype(kind)


def setup_inputs(seed: int = 0) -> dict:
    key_of = jax.random.split(jax.random.key(seed), 9)
    qkv_txt = noise(key_of[0], (BATCH, TXT, 3 * HD), 1.0, 6.0, ((0, 8), (1, 16)))
    qkv_img = draw_qkv_img(jax.random.fold_in(key_of[8], 71), 0)
    attn_img = noise_with(key_of[2], (BATCH, IMG, HD), 1.0, 6.0, ((0, 8), (1, 16)), (1, 2, 16, 2.0))
    cot_txt = noise(key_of[3], (BATCH, TXT, HD), (JOINT ** 0.5), 320.0, ((0, 8), (1, 16)))
    cot_img = noise(key_of[4], (BATCH, IMG, D), (JOINT ** 0.5), 320.0, ((0, 8), (1, 16)))
    gate = jnp.clip(1.0 + 0.18 * jax.random.normal(key_of[5], (BATCH, D), jnp.float32), 0.1, 1.9)
    advantage = noise(key_of[6], (BATCH,), 1.0, 3.0, ((0, 8),), jnp.float32)
    proj_weight = noise(key_of[7], (HD, D), HD ** -0.5, 0.125)
    return {"qkv_txt": qkv_txt, "qkv_img": qkv_img, "attn_img": attn_img, "cot_txt": cot_txt, "cot_img": cot_img, "gate": gate, "advantage": advantage, "proj_weight": proj_weight}


def head_backward(pieces):
    query_rows, key_rows, value_rows, grad_rows = pieces
    scale = HEAD_SIZE ** -0.5
    scores = jnp.dot(query_rows, key_rows.T, preferred_element_type=jnp.float32) * scale
    shifted = jnp.exp(scores - jnp.max(scores, axis=-1, keepdims=True))
    probs = shifted / jnp.sum(shifted, axis=-1, keepdims=True)
    probs_low = probs.astype(jnp.bfloat16)
    value_grad = jnp.dot(probs_low.T, grad_rows, preferred_element_type=jnp.float32)
    prob_grad = jnp.dot(grad_rows, value_rows.T, preferred_element_type=jnp.float32)
    centre = jnp.sum(probs * prob_grad, axis=-1, keepdims=True)
    score_grad = (probs * (prob_grad - centre) * scale).astype(jnp.bfloat16)
    query_grad = jnp.dot(score_grad, key_rows, preferred_element_type=jnp.float32)
    key_grad = jnp.dot(score_grad.T, query_rows, preferred_element_type=jnp.float32)
    return jnp.stack([query_grad, key_grad, value_grad]).astype(jnp.bfloat16)


def per_head(array):
    return jnp.transpose(array, (0, 2, 1, 3)).reshape(BATCH * HEADS, JOINT, HEAD_SIZE)


def reference(qkv_txt, qkv_img, attn_img, cot_txt, cot_img, gate, advantage, proj_weight):
    weighted = advantage[:, None, None] * gate[:, None, :]
    d_image = (weighted * cot_img.astype(jnp.float32)).astype(jnp.bfloat16)
    d_out_img = jnp.einsum("btd,hd->bth", d_image.astype(jnp.float32), proj_weight.astype(jnp.float32)).astype(jnp.bfloat16)
    d_out_txt = (advantage[:, None, None] * cot_txt.astype(jnp.float32)).astype(jnp.bfloat16)
    joint = jnp.concatenate([qkv_txt, qkv_img], axis=1).reshape(BATCH, JOINT, 3, HEADS, HEAD_SIZE)
    d_joint = jnp.concatenate([d_out_txt, d_out_img], axis=1).reshape(BATCH, JOINT, HEADS, HEAD_SIZE)
    grads = lax.map(head_backward, (per_head(joint[:, :, 0]), per_head(joint[:, :, 1]), per_head(joint[:, :, 2]), per_head(d_joint)))
    grads = grads.reshape(BATCH, HEADS, 3, JOINT, HEAD_SIZE)
    grads = jnp.transpose(grads, (0, 3, 2, 1, 4)).reshape(BATCH, JOINT, 3 * HD)
    grad_text = grads[:, :TXT]
    grad_image = grads[:, TXT:]
    total = jnp.dot(attn_img.reshape(BATCH * IMG, HD).T, d_image.reshape(BATCH * IMG, D), preferred_element_type=jnp.float32)
    grad_proj = total / (BATCH * IMG)
    return grad_text, grad_image, grad_proj
```

```python
import functools

import jax
import jax.numpy as jnp
from jax import lax
from jax.experimental import pallas as pl
from jax.experimental.pallas import tpu as pltpu
from jax.sharding import Mesh, PartitionSpec as P

HEAD_SIZE = 128
SCALE = HEAD_SIZE ** (-0.5)
LOG2E = 1.4426950408889634
BLOCK = 256
SEQ = ("zl", "x", "c")
PLANE = ("zh", "zl", "x")
COLUMN = ("y", "c")
BF16 = jnp.bfloat16
F32 = jnp.float32


def exchange(array, axes):
    return lax.all_to_all(array, axes, split_axis=0, concat_axis=0, tiled=True)


def params(mib):
    return pltpu.CompilerParams(vmem_limit_bytes=mib << 20)


def cost(flops, nbytes, exps=0):
    return pl.CostEstimate(flops=flops, bytes_accessed=nbytes, transcendentals=exps)


def pack_kernel(slots, *refs):
    out = refs[-1]
    txt, img = refs[:slots], refs[slots : 2 * slots]
    heads = out.shape[0]
    t = txt[0].shape[0]
    for j in range(slots):
        lanes = slice(j * HEAD_SIZE, (j + 1) * HEAD_SIZE)
        for h in range(heads):
            cols = slice(h * HEAD_SIZE, (h + 1) * HEAD_SIZE)
            out[h, :t, lanes] = txt[j][:, cols]
            out[h, t:, lanes] = img[j][:, cols]


def pack_heads(txt, img, first, slots, heads, step=4):
    t, i = txt.shape[0], img.shape[0]
    per = heads // step

    def spec(rows, j):
        return pl.BlockSpec((rows, step * HEAD_SIZE), lambda g: (0, (first + j) * per + g))

    nbytes = 2 * (t + i) * slots * heads * HEAD_SIZE * 2
    return pl.pallas_call(
        functools.partial(pack_kernel, slots),
        grid=(per,),
        in_specs=[spec(t, j) for j in range(slots)] + [spec(i, j) for j in range(slots)],
        out_specs=pl.BlockSpec((step, t + i, slots * HEAD_SIZE), lambda g: (g, 0, 0)),
        out_shape=jax.ShapeDtypeStruct((heads, t + i, slots * HEAD_SIZE), BF16),
        compiler_params=params(32),
        cost_estimate=cost(0, nbytes),
    )(*([txt] * slots), *([img] * slots))


def d_image_kernel(cot, gate, adv, out):
    weighted = adv[0, 0] * gate[...]
    value = (weighted * cot[...].astype(F32)).astype(BF16)
    groups, _, width = out.shape
    for g in range(groups):
        out[g] = value[:, g * width : (g + 1) * width]


def d_image_call(cot, gate, adv, groups):
    rows, width = cot.shape
    return pl.pallas_call(
        d_image_kernel,
        in_specs=[
            pl.BlockSpec(memory_space=pltpu.VMEM),
            pl.BlockSpec(memory_space=pltpu.VMEM),
            pl.BlockSpec(memory_space=pltpu.SMEM),
        ],
        out_specs=pl.BlockSpec(memory_space=pltpu.VMEM),
        out_shape=jax.ShapeDtypeStruct((groups, rows, width // groups), BF16),
        compiler_params=params(32),
        cost_estimate=cost(2 * rows * width, 4 * rows * width),
    )(cot, gate, adv)


def d_out_kernel(dimg, weight, cot_txt, adv, vt, vi, out):
    groups, rows, part = dimg.shape
    heads = out.shape[0]
    t = cot_txt.shape[0]
    total = jnp.zeros((rows, heads * HEAD_SIZE), F32)
    for g in range(groups):
        total += lax.dot_general(
            dimg[g],
            weight[:, g * part : (g + 1) * part],
            (((1,), (1,)), ((), ())),
            preferred_element_type=F32,
        )
    total = total.astype(BF16)
    text = (adv[0, 0] * cot_txt[...].astype(F32)).astype(BF16)
    for h in range(heads):
        cols = slice(h * HEAD_SIZE, (h + 1) * HEAD_SIZE)
        out[h, :t, :HEAD_SIZE] = vt[:, cols]
        out[h, t:, :HEAD_SIZE] = vi[:, cols]
        out[h, :t, HEAD_SIZE:] = text[:, cols]
        out[h, t:, HEAD_SIZE:] = total[:, cols]


def d_out_call(dimg, weight, cot_txt, adv, txt, img, heads, step=4):
    groups, rows, part = dimg.shape
    t = cot_txt.shape[0]
    width = step * HEAD_SIZE
    per = heads // step
    return pl.pallas_call(
        d_out_kernel,
        grid=(per,),
        in_specs=[
            pl.BlockSpec((groups, rows, part), lambda g: (0, 0, 0)),
            pl.BlockSpec((width, groups * part), lambda g: (g, 0)),
            pl.BlockSpec((t, width), lambda g: (0, g)),
            pl.BlockSpec(memory_space=pltpu.SMEM),
            pl.BlockSpec((t, width), lambda g: (0, 2 * per + g)),
            pl.BlockSpec((rows, width), lambda g: (0, 2 * per + g)),
        ],
        out_specs=pl.BlockSpec((step, t + rows, 2 * HEAD_SIZE), lambda g: (g, 0, 0)),
        out_shape=jax.ShapeDtypeStruct((heads, t + rows, 2 * HEAD_SIZE), BF16),
        compiler_params=params(40),
        cost_estimate=cost(
            2 * rows * weight.size, 2 * (weight.size + dimg.size + 3 * (t + rows) * heads * HEAD_SIZE)
        ),
    )(dimg, weight, cot_txt, adv, txt, img)


def exps_kernel(q, k, e_out, inv_out):
    scores = lax.dot_general(k[...], q[...], (((1,), (1,)), ((), ())), preferred_element_type=F32)
    top = jnp.max(scores, axis=0, keepdims=True)
    low = jnp.exp2((scores - top) * (SCALE * LOG2E)).astype(BF16)
    e_out[...] = low
    inverse = 1.0 / jnp.sum(low.astype(F32), axis=0, keepdims=True)
    inv_out[...] = jnp.transpose(jnp.broadcast_to(inverse, (HEAD_SIZE, inverse.shape[1])))


def exps_call(qk):
    n = qk.shape[0]
    return pl.pallas_call(
        exps_kernel,
        grid=(n // BLOCK,),
        in_specs=[
            pl.BlockSpec((BLOCK, HEAD_SIZE), lambda i: (i, 0)),
            pl.BlockSpec((n, HEAD_SIZE), lambda i: (0, 1)),
        ],
        out_specs=[
            pl.BlockSpec((n, BLOCK), lambda i: (0, i)),
            pl.BlockSpec((BLOCK, HEAD_SIZE), lambda i: (i, 0)),
        ],
        out_shape=[
            jax.ShapeDtypeStruct((n, n), BF16),
            jax.ShapeDtypeStruct((n, HEAD_SIZE), F32),
        ],
        compiler_params=params(56),
        cost_estimate=cost(2 * n * n * HEAD_SIZE * 2, 2 * n * n, n * n),
    )(qk, qk)


def grads_kernel(e, inv, q, k, v, d, out, dk, dv):
    step = pl.program_id(0)

    @pl.when(step == 0)
    def _():
        dk[...] = jnp.zeros_like(dk)
        dv[...] = jnp.zeros_like(dv)

    inverse = inv[...]
    d_low = (d[...].astype(F32) * inverse).astype(BF16)
    probs = e[...]
    prob_grad = lax.dot_general(v[...], d_low, (((1,), (1,)), ((), ())), preferred_element_type=F32)
    wide = probs.astype(F32)
    row = jnp.transpose(inverse)[:1]
    centre = jnp.sum(wide * prob_grad, axis=0, keepdims=True) * row
    score_grad = (wide * (prob_grad - centre)).astype(BF16)
    dv[...] += jnp.dot(probs, d_low, preferred_element_type=F32)
    dk[...] += jnp.dot(score_grad, q[...], preferred_element_type=F32)
    dq = lax.dot_general(score_grad, k[...], (((0,), (0,)), ((), ())), preferred_element_type=F32)
    rows = pl.ds(pl.multiple_of(step * BLOCK, BLOCK), BLOCK)
    out[rows, :HEAD_SIZE] = (dq * SCALE).astype(BF16)

    @pl.when(step == pl.num_programs(0) - 1)
    def _():
        out[:, HEAD_SIZE : 2 * HEAD_SIZE] = (dk[...] * SCALE).astype(BF16)
        out[:, 2 * HEAD_SIZE :] = dv[...].astype(BF16)


def grads_call(exps, inverse, qk, vd):
    n = qk.shape[0]
    block = lambda col: pl.BlockSpec((BLOCK, HEAD_SIZE), lambda i: (i, col))
    whole = lambda col: pl.BlockSpec((n, HEAD_SIZE), lambda i: (0, col))
    return pl.pallas_call(
        grads_kernel,
        grid=(n // BLOCK,),
        in_specs=[pl.BlockSpec((n, BLOCK), lambda i: (0, i)), block(0), block(0), whole(1), whole(0), block(1)],
        out_specs=pl.BlockSpec((n, 3 * HEAD_SIZE), lambda i: (0, 0)),
        out_shape=jax.ShapeDtypeStruct((n, 3 * HEAD_SIZE), BF16),
        scratch_shapes=[pltpu.VMEM((n, HEAD_SIZE), F32), pltpu.VMEM((n, HEAD_SIZE), F32)],
        compiler_params=params(56),
        cost_estimate=cost(2 * n * n * HEAD_SIZE * 8, 2 * n * n),
    )(exps, inverse, qk, qk, vd, vd)


def unpack_kernel(back, txt, img):
    t = txt.shape[0]
    for h in range(back.shape[0]):
        cols = slice(h * HEAD_SIZE, (h + 1) * HEAD_SIZE)
        txt[:, cols] = back[h, :t]
        img[:, cols] = back[h, t:]


def unpack_call(back, t):
    heads, tokens, _ = back.shape
    width = heads * HEAD_SIZE
    i = tokens - t
    return pl.pallas_call(
        unpack_kernel,
        grid=(3,),
        in_specs=[pl.BlockSpec((heads, tokens, HEAD_SIZE), lambda j: (0, 0, j))],
        out_specs=[
            pl.BlockSpec((t, width), lambda j: (0, j)),
            pl.BlockSpec((i, width), lambda j: (0, j)),
        ],
        out_shape=[
            jax.ShapeDtypeStruct((t, 3 * width), BF16),
            jax.ShapeDtypeStruct((i, 3 * width), BF16),
        ],
        compiler_params=params(32),
        cost_estimate=cost(0, 12 * tokens * width),
    )(back)


def per_device(qkv_txt, qkv_img, attn_img, cot_txt, cot_img, gate, advantage, proj_weight):
    txt, img = qkv_txt[0], qkv_img[0]
    tokens = txt.shape[0] + img.shape[0]
    width = attn_img.shape[2]
    heads = width // HEAD_SIZE
    model = cot_img.shape[2]
    adv = advantage[:, None]
    column = 1
    for name in COLUMN:
        column *= lax.axis_size(name)
    plane = 1
    for name in PLANE:
        plane *= lax.axis_size(name)

    attn = lax.all_gather(attn_img[0], COLUMN, axis=0, tiled=True)
    qk = exchange(pack_heads(txt, img, 0, 2, heads), SEQ)
    d_image = d_image_call(cot_img[0], gate, adv, column)
    vd = exchange(d_out_call(d_image, proj_weight, cot_txt[0], adv, txt, img, heads), SEQ)
    d_columns = exchange(d_image, COLUMN)

    n = heads * tokens
    qk = qk.reshape(n, 2 * HEAD_SIZE)
    vd = vd.reshape(n, 2 * HEAD_SIZE)
    exps, inverse = exps_call(qk)

    d_columns = d_columns.reshape(-1, model // column)
    product = lax.dot_general(attn, d_columns, (((0,), (0,)), ((), ())), preferred_element_type=F32)
    sizes = [lax.axis_size(name) for name in ("zh", "y", "zl", "x", "c")]
    rows = width // (column * plane)
    product = product.astype(BF16).reshape(*sizes, rows, model // column)
    product = jnp.transpose(product, (0, 2, 3, 1, 4, 5, 6)).reshape(plane, column * rows, model // column)
    product = exchange(product, PLANE)
    total = jnp.sum(product.astype(F32), axis=0) * (1.0 / (img.shape[0] * column * plane))
    total = exchange(total.reshape(column, rows, model // column), COLUMN)
    grad_proj = jnp.transpose(total, (1, 0, 2)).reshape(rows, model)

    grads = grads_call(exps, inverse, qk, vd).reshape(heads, tokens, 3 * HEAD_SIZE)
    dqkv_txt, dqkv_img = unpack_call(exchange(grads, SEQ), txt.shape[0])
    return (dqkv_txt[None], dqkv_img[None], grad_proj)


def solution(mesh):
    fine = Mesh(mesh.devices.reshape(2, 4, 2, 4, 2), ("zh", "y", "zl", "x", "c"))
    dp = ("zh", "y")
    tokens = P(dp, SEQ, None)
    return jax.shard_map(
        per_device,
        mesh=fine,
        in_specs=(tokens, tokens, tokens, tokens, tokens, P(dp, None), P(dp), P()),
        out_specs=(tokens, tokens, P(dp + SEQ, None)),
        check_vma=False,
    )
```

```python
import functools

import jax
import jax.numpy as jnp
from jax import lax
from jax.experimental import pallas as pl
from jax.experimental.pallas import tpu as pltpu
from jax.sharding import Mesh, PartitionSpec as P

HEAD_SIZE = 128
SCALE = HEAD_SIZE ** (-0.5)
LOG2E = 1.4426950408889634
BLOCK = 512
CHUNK = 256
SEQ = ("zl", "x", "c")
PLANE = ("zh", "zl", "x")
ALL = ("zh", "y", "zl", "x", "c")
BF16 = jnp.bfloat16
F32 = jnp.float32


def exchange(array, axes):
    return lax.all_to_all(array, axes, split_axis=0, concat_axis=0, tiled=True)


def params(mib):
    return pltpu.CompilerParams(vmem_limit_bytes=mib << 20)


def cost(flops, nbytes, exps=0):
    return pl.CostEstimate(flops=flops // 1000, bytes_accessed=nbytes // 1000, transcendentals=exps // 1000)


def pack_kernel(slots, *refs):
    out = refs[-1]
    txt, img = refs[:slots], refs[slots : 2 * slots]
    heads = out.shape[0]
    t = txt[0].shape[0]
    for j in range(slots):
        lanes = slice(j * HEAD_SIZE, (j + 1) * HEAD_SIZE)
        for h in range(heads):
            cols = slice(h * HEAD_SIZE, (h + 1) * HEAD_SIZE)
            out[h, :t, lanes] = txt[j][:, cols]
            out[h, t:, lanes] = img[j][:, cols]


def pack_heads(txt, img, first, slots, heads, step=4):
    t, i = txt.shape[0], img.shape[0]
    per = heads // step

    def spec(rows, j):
        return pl.BlockSpec((rows, step * HEAD_SIZE), lambda g: (0, (first + j) * per + g))

    nbytes = 2 * (t + i) * slots * heads * HEAD_SIZE * 2
    return pl.pallas_call(
        functools.partial(pack_kernel, slots),
        grid=(per,),
        in_specs=[spec(t, j) for j in range(slots)] + [spec(i, j) for j in range(slots)],
        out_specs=pl.BlockSpec((step, t + i, slots * HEAD_SIZE), lambda g: (g, 0, 0)),
        out_shape=jax.ShapeDtypeStruct((heads, t + i, slots * HEAD_SIZE), BF16),
        compiler_params=params(56),
        cost_estimate=cost(0, nbytes),
    )(*([txt] * slots), *([img] * slots))


def d_image_kernel(cot, gate, adv, y, attn, out, here, ahead, behind, across):
    weighted = adv[0, 0] * gate[...]
    out[...] = (weighted * cot[...].astype(F32)).astype(BF16)
    width = here.shape[1]
    count = out.shape[1] // width
    for hop, ref in ((0, here), (1, ahead), (count - 1, behind), (2, across)):
        start = lax.rem(y[0, 0] + hop, count) * width
        ref[:, ref.shape[1] - width :] = out[:, pl.ds(pl.multiple_of(start, width), width)]
    across[:, : attn.shape[1]] = attn[...]


def d_image_call(cot, gate, adv, y, attn, count):
    rows, width = cot.shape
    vmem = pl.BlockSpec(memory_space=pltpu.VMEM)
    smem = pl.BlockSpec(memory_space=pltpu.SMEM)
    part = jax.ShapeDtypeStruct((rows, width // count), BF16)
    return pl.pallas_call(
        d_image_kernel,
        in_specs=[vmem, vmem, smem, smem, vmem],
        out_specs=[vmem] * 5,
        out_shape=[
            jax.ShapeDtypeStruct((rows, width), BF16),
            part,
            part,
            part,
            jax.ShapeDtypeStruct((rows, width // count + attn.shape[1]), BF16),
        ],
        compiler_params=params(56),
        cost_estimate=cost(2 * rows * width, 6 * rows * width),
    )(cot, gate, adv, y, attn)


def partial_kernel(c, a0, a1, a2, d0, d1, d2, merged, keep, low, high):
    block, half = keep.shape
    at = pl.program_id(0) * block
    rows = merged.shape[1] - 2 * half
    lhs = [a0[...], a1[...], a2[...], merged[:, pl.ds(pl.multiple_of(at, block), block)]]
    rhs = [d0[...], d1[...], d2[...], merged[:, rows:]]
    value = lax.dot_general(
        jnp.concatenate(lhs, axis=0),
        jnp.concatenate(rhs, axis=0),
        (((0,), (0,)), ((), ())),
        preferred_element_type=F32,
    )
    left, right = value[:, :half], value[:, half:]
    first = c[0, 0] == 0
    keep[...] = jnp.where(first, left, right).astype(BF16)
    send = jnp.where(first, right, left).astype(BF16)
    early = pl.program_id(0) < pl.num_programs(0) // 2

    @pl.when(early)
    def _():
        low[...] = send

    @pl.when(jnp.logical_not(early))
    def _():
        high[...] = send


def partial_call(c, attns, parts, merged):
    tokens, rows = attns[0].shape
    cols = parts[0].shape[1]
    block = 512
    a_spec = pl.BlockSpec((tokens, block), lambda i: (0, i))
    d_spec = pl.BlockSpec((tokens, cols), lambda i: (0, 0))
    m_spec = pl.BlockSpec((tokens, rows + cols), lambda i: (0, 0))
    half = rows // block // 2
    out = pl.BlockSpec((block, cols // 2), lambda i: (i, 0))
    return pl.pallas_call(
        partial_kernel,
        grid=(rows // block,),
        in_specs=[pl.BlockSpec(memory_space=pltpu.SMEM)] + [a_spec] * 3 + [d_spec] * 3 + [m_spec],
        out_specs=[
            out,
            pl.BlockSpec((block, cols // 2), lambda i: (jnp.minimum(i, half - 1), 0)),
            pl.BlockSpec((block, cols // 2), lambda i: (jnp.maximum(i - half, 0), 0)),
        ],
        out_shape=[
            jax.ShapeDtypeStruct((rows, cols // 2), BF16),
            jax.ShapeDtypeStruct((rows // 2, cols // 2), BF16),
            jax.ShapeDtypeStruct((rows // 2, cols // 2), BF16),
        ],
        compiler_params=params(40),
        cost_estimate=cost(8 * tokens * rows * cols, 8 * tokens * (rows + cols) + 2 * rows * cols),
    )(c, *attns, *parts, merged)


def place_kernel(ring, keep, low, high, out):
    places, rows, _ = out.shape
    got = jnp.where(pl.program_id(0) == 0, low[...], high[...])
    value = (keep[...].astype(F32) + got.astype(F32)).astype(BF16)
    rows //= ring
    for y in range(ring):
        for place in range(places):
            at = (y * places + place) * rows
            out[place, y * rows : (y + 1) * rows] = value[at : at + rows]


def place_call(keep, got, ring, places, rows):
    cols = keep.shape[1]
    block = pl.BlockSpec((ring * places * rows, cols), lambda h: (h, 0))
    return pl.pallas_call(
        functools.partial(place_kernel, ring),
        grid=(len(got),),
        in_specs=[block] + [pl.BlockSpec((ring * places * rows, cols), lambda h: (0, 0))] * len(got),
        out_specs=pl.BlockSpec((places, ring * rows, cols), lambda h: (h, 0, 0)),
        out_shape=jax.ShapeDtypeStruct((len(got) * places, ring * rows, cols), BF16),
        compiler_params=params(24),
        cost_estimate=cost(0, 6 * keep.size),
    )(keep, *got)


def d_out_kernel(dimg, weight, cot_txt, adv, vt, vi, out):
    heads = out.shape[0]
    t = cot_txt.shape[0]
    total = lax.dot_general(dimg[...], weight[...], (((1,), (1,)), ((), ())), preferred_element_type=F32)
    total = total.astype(BF16)
    text = (adv[0, 0] * cot_txt[...].astype(F32)).astype(BF16)
    for h in range(heads):
        cols = slice(h * HEAD_SIZE, (h + 1) * HEAD_SIZE)
        out[h, :t, :HEAD_SIZE] = vt[:, cols]
        out[h, t:, :HEAD_SIZE] = vi[:, cols]
        out[h, :t, HEAD_SIZE:] = text[:, cols]
        out[h, t:, HEAD_SIZE:] = total[:, cols]


def d_out_call(dimg, weight, cot_txt, adv, txt, img, heads, step=4):
    rows, model = dimg.shape
    t = cot_txt.shape[0]
    width = step * HEAD_SIZE
    per = heads // step
    return pl.pallas_call(
        d_out_kernel,
        grid=(per,),
        in_specs=[
            pl.BlockSpec((rows, model), lambda g: (0, 0)),
            pl.BlockSpec((width, model), lambda g: (g, 0)),
            pl.BlockSpec((t, width), lambda g: (0, g)),
            pl.BlockSpec(memory_space=pltpu.SMEM),
            pl.BlockSpec((t, width), lambda g: (0, 2 * per + g)),
            pl.BlockSpec((rows, width), lambda g: (0, 2 * per + g)),
        ],
        out_specs=pl.BlockSpec((step, t + rows, 2 * HEAD_SIZE), lambda g: (g, 0, 0)),
        out_shape=jax.ShapeDtypeStruct((heads, t + rows, 2 * HEAD_SIZE), BF16),
        compiler_params=params(56),
        cost_estimate=cost(
            2 * rows * weight.size, 2 * (weight.size + dimg.size + 3 * (t + rows) * heads * HEAD_SIZE)
        ),
    )(dimg, weight, cot_txt, adv, txt, img)


def fold(array, combine):
    return combine(array.reshape(-1, 8, array.shape[1]), axis=0)


def exps_kernel(q, k, e_out, inv_out, scores):
    chunks = [slice(at, at + CHUNK) for at in range(0, k.shape[0], CHUNK)]
    top = None
    for rows in chunks:
        part = lax.dot_general(k[rows], q[...], (((1,), (1,)), ((), ())), preferred_element_type=F32)
        scores[rows] = part
        part = fold(part, jnp.max)
        top = part if top is None else jnp.maximum(top, part)
    top = jnp.max(top, axis=0, keepdims=True)
    total = jnp.zeros((8, top.shape[1]), F32)
    for rows in chunks:
        low = jnp.exp2((scores[rows] - top) * (SCALE * LOG2E)).astype(BF16)
        e_out[rows] = low
        total += fold(low.astype(F32), jnp.sum)
    inverse = 1.0 / jnp.sum(total, axis=0, keepdims=True)
    inv_out[...] = jnp.transpose(jnp.broadcast_to(inverse, (HEAD_SIZE, inverse.shape[1])))


def exps_call(qk):
    n = qk.shape[0]
    block = BLOCK
    return pl.pallas_call(
        exps_kernel,
        grid=(n // block,),
        in_specs=[
            pl.BlockSpec((block, HEAD_SIZE), lambda i: (i, 0)),
            pl.BlockSpec((n, HEAD_SIZE), lambda i: (0, 1)),
        ],
        out_specs=[
            pl.BlockSpec((n, block), lambda i: (0, i)),
            pl.BlockSpec((block, HEAD_SIZE), lambda i: (i, 0)),
        ],
        out_shape=[
            jax.ShapeDtypeStruct((n, n), BF16),
            jax.ShapeDtypeStruct((n, HEAD_SIZE), F32),
        ],
        scratch_shapes=[pltpu.VMEM((n, block), F32)],
        compiler_params=params(56),
        cost_estimate=cost(2 * n * n * HEAD_SIZE * 2, 2 * n * n, n * n),
    )(qk, qk)


def grads_kernel(e, inv, q, k, v, d, out, dk, dv, prob_grads):
    step = pl.program_id(0)
    chunks = [slice(at, at + CHUNK) for at in range(0, k.shape[0], CHUNK)]

    @pl.when(step == 0)
    def _():
        dk[...] = jnp.zeros_like(dk)
        dv[...] = jnp.zeros_like(dv)

    inverse = inv[...]
    d_low = (d[...].astype(F32) * inverse).astype(BF16)
    centre = jnp.zeros((8, BLOCK), F32)
    for rows in chunks:
        probs = e[rows]
        part = lax.dot_general(v[rows], d_low, (((1,), (1,)), ((), ())), preferred_element_type=F32)
        prob_grads[rows] = part
        centre += fold(probs.astype(F32) * part, jnp.sum)
        dv[rows] += jnp.dot(probs, d_low, preferred_element_type=F32)
    centre = jnp.sum(centre, axis=0, keepdims=True) * jnp.transpose(inverse)[:1]
    dq = jnp.zeros((BLOCK, HEAD_SIZE), F32)
    for rows in chunks:
        score_grad = (e[rows].astype(F32) * (prob_grads[rows] - centre)).astype(BF16)
        dk[rows] += jnp.dot(score_grad, q[...], preferred_element_type=F32)
        dq += lax.dot_general(score_grad, k[rows], (((0,), (0,)), ((), ())), preferred_element_type=F32)
    out[pl.ds(pl.multiple_of(step * BLOCK, BLOCK), BLOCK), :HEAD_SIZE] = (dq * SCALE).astype(BF16)

    @pl.when(step == pl.num_programs(0) - 1)
    def _():
        out[:, HEAD_SIZE : 2 * HEAD_SIZE] = (dk[...] * SCALE).astype(BF16)
        out[:, 2 * HEAD_SIZE :] = dv[...].astype(BF16)


def grads_call(exps, inverse, qk, vd):
    n = qk.shape[0]
    block = lambda col: pl.BlockSpec((BLOCK, HEAD_SIZE), lambda i: (i, col))
    whole = lambda col: pl.BlockSpec((n, HEAD_SIZE), lambda i: (0, col))
    return pl.pallas_call(
        grads_kernel,
        grid=(n // BLOCK,),
        in_specs=[pl.BlockSpec((n, BLOCK), lambda i: (0, i)), block(0), block(0), whole(1), whole(0), block(1)],
        out_specs=pl.BlockSpec((n, 3 * HEAD_SIZE), lambda i: (0, 0)),
        out_shape=jax.ShapeDtypeStruct((n, 3 * HEAD_SIZE), BF16),
        scratch_shapes=[pltpu.VMEM((n, HEAD_SIZE), F32)] * 2 + [pltpu.VMEM((n, BLOCK), F32)],
        compiler_params=params(56),
        cost_estimate=cost(2 * n * n * HEAD_SIZE * 8, 2 * n * n),
    )(exps, inverse, qk, qk, vd, vd)


def unpack_kernel(back, txt, img):
    t = txt.shape[0]
    for h in range(back.shape[0]):
        cols = slice(h * HEAD_SIZE, (h + 1) * HEAD_SIZE)
        txt[:, cols] = back[h, :t]
        img[:, cols] = back[h, t:]


def unpack_call(back, t):
    heads, tokens, _ = back.shape
    width = heads * HEAD_SIZE
    i = tokens - t
    return pl.pallas_call(
        unpack_kernel,
        grid=(3,),
        in_specs=[pl.BlockSpec((heads, tokens, HEAD_SIZE), lambda j: (0, 0, j))],
        out_specs=[
            pl.BlockSpec((t, width), lambda j: (0, j)),
            pl.BlockSpec((i, width), lambda j: (0, j)),
        ],
        out_shape=[
            jax.ShapeDtypeStruct((t, 3 * width), BF16),
            jax.ShapeDtypeStruct((i, 3 * width), BF16),
        ],
        compiler_params=params(24),
        cost_estimate=cost(0, 12 * tokens * width),
    )(back)


def ring_kernel(y, *refs):
    out = refs[-1]
    count = len(refs) - 1
    width = refs[0].shape[1]
    for hop in range(count):
        start = lax.rem(y[0, 0] + count - hop, count) * width
        out[:, pl.ds(pl.multiple_of(start, width), width)] = refs[hop][...]


def ring_call(y, pieces):
    rows, width = pieces[0].shape
    vmem = pl.BlockSpec(memory_space=pltpu.VMEM)
    return pl.pallas_call(
        ring_kernel,
        in_specs=[pl.BlockSpec(memory_space=pltpu.SMEM)] + [vmem] * len(pieces),
        out_specs=vmem,
        out_shape=jax.ShapeDtypeStruct((rows, width * len(pieces)), F32),
        compiler_params=params(16),
        cost_estimate=cost(0, 8 * rows * width * len(pieces)),
    )(y, *pieces)


def per_device(qkv_txt, qkv_img, attn_img, cot_txt, cot_img, gate, advantage, proj_weight):
    txt, img = qkv_txt[0], qkv_img[0]
    tokens = txt.shape[0] + img.shape[0]
    width = attn_img.shape[2]
    heads = width // HEAD_SIZE
    model = cot_img.shape[2]
    adv = advantage[:, None]
    count = lax.axis_size("y")
    y = lax.axis_index("y").astype(jnp.int32)
    c = lax.axis_index("c").astype(jnp.int32)
    hops = (1, count - 1, 2)

    def shift(array, hop):
        return lax.ppermute(array, "y", [(i, (i + hop) % count) for i in range(count)])

    def swap(array):
        return lax.ppermute(array, "c", [(0, 1), (1, 0)])

    attn = attn_img[0]
    packed = pack_heads(txt, img, 0, 2, heads)
    qk = exchange(packed, SEQ)
    cot, attn, packed = lax.optimization_barrier((cot_img[0], attn, packed))
    attns = [shift(attn, hop) for hop in hops[:2]]
    d_image, here, *parts = d_image_call(cot, gate, adv, y.reshape(1, 1), attn, count)
    *parts, merged = [shift(part, hop) for hop, part in zip(hops, parts)]
    vd = d_out_call(d_image, proj_weight, cot_txt[0], adv, txt, img, heads)
    vd, qk = lax.optimization_barrier((vd, qk))
    vd = exchange(vd, SEQ)

    n = heads * tokens
    qk = qk.reshape(n, 2 * HEAD_SIZE)
    exps, inverse = exps_call(qk)
    attn, attns, here, parts, merged, inverse = lax.optimization_barrier(
        (attn, attns, here, parts, merged, inverse)
    )
    keep, *send = partial_call(c.reshape(1, 1), [attn, *attns], [here, *parts], merged)
    got = [swap(part) for part in send]

    devices = lax.axis_size(ALL)
    rows = width // devices
    cols = keep.shape[1]
    product = place_call(keep, got, count, lax.axis_size(PLANE) // 2, 2 * rows)
    product = exchange(product, PLANE)

    vd = vd.reshape(n, 2 * HEAD_SIZE)
    grads = grads_call(exps, inverse, qk, vd).reshape(heads, tokens, 3 * HEAD_SIZE)
    grads, product = lax.optimization_barrier((grads, product))
    back = exchange(grads, SEQ)

    total = jnp.sum(product.astype(F32), axis=0) * (1.0 / (img.shape[0] * devices))
    total = total.reshape(count, 2, rows, cols)
    own = lax.dynamic_index_in_dim(total, c, 1, keepdims=False)
    other = swap(lax.dynamic_index_in_dim(total, 1 - c, 1, keepdims=False))
    wide = jnp.where(c == 0, jnp.concatenate([own, other], -1), jnp.concatenate([other, own], -1))
    pick = lambda hop: lax.dynamic_index_in_dim(wide, (y + hop) % count, 0, keepdims=False)
    placed = [pick(0)] + [shift(pick(hop), hop) for hop in hops]
    order = [placed[0], placed[1], placed[3], placed[2]]
    grad_proj = ring_call(y.reshape(1, 1), order)
    back, grad_proj = lax.optimization_barrier((back, grad_proj))

    dqkv_txt, dqkv_img = unpack_call(back, txt.shape[0])
    return (dqkv_txt[None], dqkv_img[None], grad_proj)


def solution(mesh):
    fine = Mesh(mesh.devices.reshape(2, 4, 2, 4, 2), ALL)
    dp = ("zh", "y")
    tokens = P(dp, SEQ, None)
    return jax.shard_map(
        per_device,
        mesh=fine,
        in_specs=(tokens, tokens, tokens, tokens, tokens, P(dp, None), P(dp), P()),
        out_specs=(tokens, tokens, P(dp + SEQ, None)),
        check_vma=False,
    )
```

```python
import functools

import jax
import jax.numpy as jnp
from jax import lax
from jax.experimental import pallas as pl
from jax.experimental.pallas import tpu as pltpu
from jax.sharding import Mesh, PartitionSpec as P

HEAD_SIZE = 128
SCALE = HEAD_SIZE ** (-0.5)
LOG2E = 1.4426950408889634
BLOCK = 512
CHUNK = 256
SMALL = 1000
SEQ = ("zl", "x", "c")
ALL = ("zh", "y", "zl", "x", "c")
PLANE = ("zh", "zl", "x")
RING = 4
HOPS = (1, RING - 1, 2)
BF16 = jnp.bfloat16
F32 = jnp.float32


def exchange(array, axes):
    return lax.all_to_all(array, axes, split_axis=0, concat_axis=0, tiled=True)


def params(mib):
    return pltpu.CompilerParams(vmem_limit_bytes=mib << 20)


def cost(flops, nbytes, part=1):
    return pl.CostEstimate(flops=flops // part, bytes_accessed=nbytes // part, transcendentals=0)


def pack_kernel(slots, *refs):
    out = refs[-1]
    txt, img = refs[:slots], refs[slots : 2 * slots]
    heads = out.shape[0]
    t = txt[0].shape[0]
    for j in range(slots):
        lanes = slice(j * HEAD_SIZE, (j + 1) * HEAD_SIZE)
        for h in range(heads):
            cols = slice(h * HEAD_SIZE, (h + 1) * HEAD_SIZE)
            out[h, :t, lanes] = txt[j][:, cols]
            out[h, t:, lanes] = img[j][:, cols]


def pack_heads(txt, img, first, slots, heads, step=8):
    t, i = txt.shape[0], img.shape[0]
    per = heads // step

    def spec(rows, j):
        return pl.BlockSpec((rows, step * HEAD_SIZE), lambda g: (0, (first + j) * per + g))

    nbytes = 2 * (t + i) * slots * heads * HEAD_SIZE * 2
    return pl.pallas_call(
        functools.partial(pack_kernel, slots),
        grid=(per,),
        in_specs=[spec(t, j) for j in range(slots)] + [spec(i, j) for j in range(slots)],
        out_specs=pl.BlockSpec((step, t + i, slots * HEAD_SIZE), lambda g: (g, 0, 0)),
        out_shape=jax.ShapeDtypeStruct((heads, t + i, slots * HEAD_SIZE), BF16),
        compiler_params=params(56),
        cost_estimate=cost(0, nbytes),
    )(*([txt] * slots), *([img] * slots))


def d_image_kernel(cot, gate, adv, y, attn, out, here, ahead, behind, across):
    weighted = adv[0, 0] * gate[...]
    out[...] = (weighted * cot[...].astype(F32)).astype(BF16)
    width = here.shape[1]
    rows = attn.shape[1]
    count = out.shape[1] // width

    def part(hop):
        start = lax.rem(y[0, 0] + hop, count) * width
        return out[:, pl.ds(pl.multiple_of(start, width), width)]

    here[...] = part(0)
    for hop, ref in ((1, ahead), (count - 1, behind), (2, across)):
        ref[:, :rows] = attn[...]
        ref[:, rows:] = part(hop)


def d_image_call(cot, gate, adv, y, attn, count):
    rows, width = cot.shape
    part = width // count
    vmem = pl.BlockSpec(memory_space=pltpu.VMEM)
    smem = pl.BlockSpec(memory_space=pltpu.SMEM)
    return pl.pallas_call(
        d_image_kernel,
        in_specs=[vmem, vmem, smem, smem, vmem],
        out_specs=[vmem] * 5,
        out_shape=[jax.ShapeDtypeStruct((rows, width), BF16), jax.ShapeDtypeStruct((rows, part), BF16)]
        + [jax.ShapeDtypeStruct((rows, attn.shape[1] + part), BF16)] * 3,
        compiler_params=params(48),
        cost_estimate=cost(2 * rows * width, 6 * rows * width),
    )(cot, gate, adv, y, attn)


def partial_kernel(c, attn, here, m1, m2, m3, keep, low, high):
    block, half = keep.shape
    rows = m1.shape[1] - 2 * half
    at = pl.ds(pl.multiple_of(pl.program_id(0) * block, block), block)
    merged = (m1, m2, m3)
    value = lax.dot_general(
        jnp.concatenate([attn[...]] + [ref[:, at] for ref in merged], axis=0),
        jnp.concatenate([here[...]] + [ref[:, rows:] for ref in merged], axis=0),
        (((0,), (0,)), ((), ())),
        preferred_element_type=F32,
    )
    left, right = value[:, :half], value[:, half:]
    first = c[0, 0] == 0
    keep[...] = jnp.where(first, left, right).astype(BF16)
    send = jnp.where(first, right, left).astype(BF16)
    early = pl.program_id(0) < pl.num_programs(0) // 2

    @pl.when(early)
    def _():
        low[...] = send

    @pl.when(jnp.logical_not(early))
    def _():
        high[...] = send


def partial_call(c, attn, here, merged):
    tokens, rows = attn.shape
    cols = here.shape[1]
    block = 512
    half = rows // block // 2
    out = (block, cols // 2)
    return pl.pallas_call(
        partial_kernel,
        grid=(rows // block,),
        in_specs=[
            pl.BlockSpec(memory_space=pltpu.SMEM),
            pl.BlockSpec((tokens, block), lambda i: (0, i)),
            pl.BlockSpec((tokens, cols), lambda i: (0, 0)),
        ]
        + [pl.BlockSpec((tokens, rows + cols), lambda i: (0, 0))] * 3,
        out_specs=[
            pl.BlockSpec(out, lambda i: (i, 0)),
            pl.BlockSpec(out, lambda i: (jnp.minimum(i, half - 1), 0)),
            pl.BlockSpec(out, lambda i: (jnp.maximum(i - half, 0), 0)),
        ],
        out_shape=[
            jax.ShapeDtypeStruct((rows, cols // 2), BF16),
            jax.ShapeDtypeStruct((rows // 2, cols // 2), BF16),
            jax.ShapeDtypeStruct((rows // 2, cols // 2), BF16),
        ],
        compiler_params=params(40),
        cost_estimate=cost(8 * tokens * rows * cols, 8 * tokens * (rows + cols) + 2 * rows * cols, SMALL),
    )(c, attn, here, *merged)


def place_kernel(ring, keep, low, high, out):
    places, rows, _ = out.shape
    got = jnp.where(pl.program_id(0) == 0, low[...], high[...])
    value = (keep[...].astype(F32) + got.astype(F32)).astype(BF16)
    rows //= ring
    for y in range(ring):
        for place in range(places):
            at = (y * places + place) * rows
            out[place, y * rows : (y + 1) * rows] = value[at : at + rows]


def place_call(keep, got, ring, places, rows):
    cols = keep.shape[1]
    block = pl.BlockSpec((ring * places * rows, cols), lambda h: (h, 0))
    return pl.pallas_call(
        functools.partial(place_kernel, ring),
        grid=(len(got),),
        in_specs=[block] + [pl.BlockSpec((ring * places * rows, cols), lambda h: (0, 0))] * len(got),
        out_specs=pl.BlockSpec((places, ring * rows, cols), lambda h: (h, 0, 0)),
        out_shape=jax.ShapeDtypeStruct((len(got) * places, ring * rows, cols), BF16),
        compiler_params=params(40),
        cost_estimate=cost(0, 6 * keep.size, SMALL),
    )(keep, *got)


def ring_kernel(y, *refs):
    out = refs[-1]
    count = len(refs) - 1
    width = refs[0].shape[1]
    for hop in range(count):
        start = lax.rem(y[0, 0] + count - hop, count) * width
        out[:, pl.ds(pl.multiple_of(start, width), width)] = refs[hop][...]


def ring_call(y, pieces):
    rows, width = pieces[0].shape
    vmem = pl.BlockSpec(memory_space=pltpu.VMEM)
    return pl.pallas_call(
        ring_kernel,
        in_specs=[pl.BlockSpec(memory_space=pltpu.SMEM)] + [vmem] * len(pieces),
        out_specs=vmem,
        out_shape=jax.ShapeDtypeStruct((rows, width * len(pieces)), F32),
        compiler_params=params(16),
        cost_estimate=cost(0, 8 * rows * width * len(pieces), SMALL),
    )(y, *pieces)


def d_out_kernel(dimg, weight, cot_txt, adv, vt, vi, out):
    heads = out.shape[0]
    t = cot_txt.shape[0]
    total = lax.dot_general(dimg[...], weight[...], (((1,), (1,)), ((), ())), preferred_element_type=F32)
    total = total.astype(BF16)
    text = (adv[0, 0] * cot_txt[...].astype(F32)).astype(BF16)
    for h in range(heads):
        cols = slice(h * HEAD_SIZE, (h + 1) * HEAD_SIZE)
        out[h, :t, :HEAD_SIZE] = vt[:, cols]
        out[h, t:, :HEAD_SIZE] = vi[:, cols]
        out[h, :t, HEAD_SIZE:] = text[:, cols]
        out[h, t:, HEAD_SIZE:] = total[:, cols]


def d_out_call(dimg, weight, cot_txt, adv, txt, img, heads, step=4):
    rows, model = dimg.shape
    t = cot_txt.shape[0]
    width = step * HEAD_SIZE
    per = heads // step
    return pl.pallas_call(
        d_out_kernel,
        grid=(per,),
        in_specs=[
            pl.BlockSpec((rows, model), lambda g: (0, 0)),
            pl.BlockSpec((width, model), lambda g: (g, 0)),
            pl.BlockSpec((t, width), lambda g: (0, g)),
            pl.BlockSpec(memory_space=pltpu.SMEM),
            pl.BlockSpec((t, width), lambda g: (0, 2 * per + g)),
            pl.BlockSpec((rows, width), lambda g: (0, 2 * per + g)),
        ],
        out_specs=pl.BlockSpec((step, t + rows, 2 * HEAD_SIZE), lambda g: (g, 0, 0)),
        out_shape=jax.ShapeDtypeStruct((heads, t + rows, 2 * HEAD_SIZE), BF16),
        compiler_params=params(51),
        cost_estimate=cost(
            2 * rows * weight.size, 2 * (weight.size + dimg.size + 3 * (t + rows) * heads * HEAD_SIZE)
        ),
    )(dimg, weight, cot_txt, adv, txt, img)


def fold(array, combine):
    return combine(array.reshape(-1, 8, array.shape[1]), axis=0)


def exps_kernel(q, k, e_out, inv_out, scores):
    chunks = [slice(at, at + CHUNK) for at in range(0, k.shape[0], CHUNK)]
    top = None
    for rows in chunks:
        part = lax.dot_general(k[rows], q[...], (((1,), (1,)), ((), ())), preferred_element_type=F32)
        scores[rows] = part
        part = fold(part, jnp.max)
        top = part if top is None else jnp.maximum(top, part)
    top = jnp.max(top, axis=0, keepdims=True)
    total = jnp.zeros((8, top.shape[1]), F32)
    for rows in chunks:
        low = jnp.exp2((scores[rows] - top) * (SCALE * LOG2E)).astype(BF16)
        e_out[rows] = low
        total += fold(low.astype(F32), jnp.sum)
    inverse = 1.0 / jnp.sum(total, axis=0, keepdims=True)
    inv_out[...] = jnp.transpose(jnp.broadcast_to(inverse, (HEAD_SIZE, inverse.shape[1])))


def exps_call(qk):
    n = qk.shape[0]
    block = BLOCK
    return pl.pallas_call(
        exps_kernel,
        grid=(n // block,),
        in_specs=[
            pl.BlockSpec((block, HEAD_SIZE), lambda i: (i, 0)),
            pl.BlockSpec((n, HEAD_SIZE), lambda i: (0, 1)),
        ],
        out_specs=[
            pl.BlockSpec((n, block), lambda i: (0, i)),
            pl.BlockSpec((block, HEAD_SIZE), lambda i: (i, 0)),
        ],
        out_shape=[
            jax.ShapeDtypeStruct((n, n), BF16),
            jax.ShapeDtypeStruct((n, HEAD_SIZE), F32),
        ],
        scratch_shapes=[pltpu.VMEM((n, block), F32)],
        compiler_params=params(56),
        cost_estimate=cost(2 * n * n * HEAD_SIZE * 2, 2 * n * n, SMALL),
    )(qk, qk)


def grads_kernel(e, inv, q, k, v, d, out, dk, dv, prob_grads):
    step = pl.program_id(0)
    chunks = [slice(at, at + CHUNK) for at in range(0, k.shape[0], CHUNK)]

    @pl.when(step == 0)
    def _():
        dk[...] = jnp.zeros_like(dk)
        dv[...] = jnp.zeros_like(dv)

    inverse = inv[...]
    d_low = (d[...].astype(F32) * inverse).astype(BF16)
    centre = jnp.zeros((8, BLOCK), F32)
    for rows in chunks:
        probs = e[rows]
        part = lax.dot_general(v[rows], d_low, (((1,), (1,)), ((), ())), preferred_element_type=F32)
        prob_grads[rows] = part
        centre += fold(probs.astype(F32) * part, jnp.sum)
        dv[rows] += jnp.dot(probs, d_low, preferred_element_type=F32)
    centre = jnp.sum(centre, axis=0, keepdims=True) * jnp.transpose(inverse)[:1]
    dq = jnp.zeros((BLOCK, HEAD_SIZE), F32)
    for rows in chunks:
        score_grad = (e[rows].astype(F32) * (prob_grads[rows] - centre)).astype(BF16)
        dk[rows] += jnp.dot(score_grad, q[...], preferred_element_type=F32)
        dq += lax.dot_general(score_grad, k[rows], (((0,), (0,)), ((), ())), preferred_element_type=F32)
    out[pl.ds(pl.multiple_of(step * BLOCK, BLOCK), BLOCK), :HEAD_SIZE] = (dq * SCALE).astype(BF16)

    @pl.when(step == pl.num_programs(0) - 1)
    def _():
        out[:, HEAD_SIZE : 2 * HEAD_SIZE] = (dk[...] * SCALE).astype(BF16)
        out[:, 2 * HEAD_SIZE :] = dv[...].astype(BF16)


def grads_call(exps, inverse, qk, vd):
    n = qk.shape[0]
    block = lambda col: pl.BlockSpec((BLOCK, HEAD_SIZE), lambda i: (i, col))
    whole = lambda col: pl.BlockSpec((n, HEAD_SIZE), lambda i: (0, col))
    return pl.pallas_call(
        grads_kernel,
        grid=(n // BLOCK,),
        in_specs=[pl.BlockSpec((n, BLOCK), lambda i: (0, i)), block(0), block(0), whole(1), whole(0), block(1)],
        out_specs=pl.BlockSpec((n, 3 * HEAD_SIZE), lambda i: (0, 0)),
        out_shape=jax.ShapeDtypeStruct((n, 3 * HEAD_SIZE), BF16),
        scratch_shapes=[pltpu.VMEM((n, HEAD_SIZE), F32)] * 2 + [pltpu.VMEM((n, BLOCK), F32)],
        compiler_params=params(56),
        cost_estimate=cost(2 * n * n * HEAD_SIZE * 8, 2 * n * n, SMALL),
    )(exps, inverse, qk, qk, vd, vd)


def unpack_kernel(back, txt, img):
    t = txt.shape[0]
    for h in range(back.shape[0]):
        cols = slice(h * HEAD_SIZE, (h + 1) * HEAD_SIZE)
        txt[:, cols] = back[h, :t]
        img[:, cols] = back[h, t:]


def unpack_call(back, t):
    heads, tokens, _ = back.shape
    width = heads * HEAD_SIZE
    i = tokens - t
    return pl.pallas_call(
        unpack_kernel,
        grid=(3,),
        in_specs=[pl.BlockSpec((heads, tokens, HEAD_SIZE), lambda j: (0, 0, j))],
        out_specs=[
            pl.BlockSpec((t, width), lambda j: (0, j)),
            pl.BlockSpec((i, width), lambda j: (0, j)),
        ],
        out_shape=[
            jax.ShapeDtypeStruct((t, 3 * width), BF16),
            jax.ShapeDtypeStruct((i, 3 * width), BF16),
        ],
        compiler_params=params(24),
        cost_estimate=cost(0, 12 * tokens * width, SMALL),
    )(back)


def per_device(qkv_txt, qkv_img, attn_img, cot_txt, cot_img, gate, advantage, proj_weight):
    txt, img = qkv_txt[0], qkv_img[0]
    tokens = txt.shape[0] + img.shape[0]
    width = attn_img.shape[2]
    heads = width // HEAD_SIZE
    model = cot_img.shape[2]
    adv = advantage[:, None]
    index = lambda axes: lax.axis_index(axes).astype(jnp.int32).reshape(1, 1)
    y, core = index("y"), index("c")

    def shift(arrays, axes):
        perms = [[(i, (i + hop) % RING) for i in range(RING)] for hop in HOPS]
        return [lax.ppermute(array, axes, perm) for array, perm in zip(arrays, perms)]

    def swap(array):
        return lax.ppermute(array, "c", [(0, 1), (1, 0)])

    attn = attn_img[0]
    packed = pack_heads(txt, img, 0, 2, heads)
    qk = exchange(packed, SEQ)
    cot, attn, packed = lax.optimization_barrier((cot_img[0], attn, packed))
    d_image, here, *merged = d_image_call(cot, gate, adv, y, attn, RING)
    merged = shift(merged, "y")
    vd = d_out_call(d_image, proj_weight, cot_txt[0], adv, txt, img, heads)
    vd, qk = lax.optimization_barrier((vd, qk))
    vd = exchange(vd, SEQ)

    n = heads * tokens
    qk = qk.reshape(n, 2 * HEAD_SIZE)
    exps, inverse = exps_call(qk)
    attn, here, merged, inverse = lax.optimization_barrier((attn, here, merged, inverse))
    keep, low, high = partial_call(core, attn, here, merged)
    low, high = swap(low), swap(high)

    devices = lax.axis_size(ALL)
    rows = width // devices
    cols = keep.shape[1]
    product = place_call(keep, [low, high], RING, lax.axis_size(PLANE) // 2, 2 * rows)
    product = exchange(product, PLANE)

    vd = vd.reshape(n, 2 * HEAD_SIZE)
    grads = grads_call(exps, inverse, qk, vd).reshape(heads, tokens, 3 * HEAD_SIZE)
    grads, product = lax.optimization_barrier((grads, product))
    back = exchange(grads, SEQ)

    total = jnp.sum(product.astype(F32), axis=0) * (1.0 / (img.shape[0] * devices))
    total = total.reshape(RING, 2, rows, cols)
    c, y = core[0, 0], y[0, 0]
    own = lax.dynamic_index_in_dim(total, c, 1, keepdims=False)
    other = swap(lax.dynamic_index_in_dim(total, 1 - c, 1, keepdims=False))
    wide = jnp.where(c == 0, jnp.concatenate([own, other], -1), jnp.concatenate([other, own], -1))
    pick = lambda hop: lax.dynamic_index_in_dim(wide, (y + hop) % RING, 0, keepdims=False)
    behind, ahead, across = shift([pick(hop) for hop in HOPS], "y")
    grad_proj = ring_call(y.reshape(1, 1), [pick(0), behind, across, ahead])
    back, grad_proj = lax.optimization_barrier((back, grad_proj))

    dqkv_txt, dqkv_img = unpack_call(back, txt.shape[0])
    return (dqkv_txt[None], dqkv_img[None], grad_proj)


def solution(mesh):
    fine = Mesh(mesh.devices.reshape(2, 4, 2, 4, 2), ALL)
    dp = ("zh", "y")
    tokens = P(dp, SEQ, None)
    return jax.shard_map(
        per_device,
        mesh=fine,
        in_specs=(tokens, tokens, tokens, tokens, tokens, P(dp, None), P(dp), P()),
        out_specs=(tokens, tokens, P(dp + SEQ, None)),
        check_vma=False,
    )
```

```python
import functools

import jax
import jax.numpy as jnp
from jax import lax
from jax.experimental import pallas as pl
from jax.experimental.pallas import tpu as pltpu
from jax.sharding import Mesh, PartitionSpec as P

HEAD_SIZE = 128
SCALE = HEAD_SIZE ** (-0.5)
LOG2E = 1.4426950408889634
BLOCK = 512
CHUNK = 256
SMALL = 1000
SAFE = 2.0**40
SEQ = ("zl", "x", "c")
ALL = ("zh", "y", "zl", "x", "c")
PLANE = ("zh", "zl", "x")
RING = 4
HOPS = (1, RING - 1, 2)
BF16 = jnp.bfloat16
F32 = jnp.float32


def exchange(array, axes):
    return lax.all_to_all(array, axes, split_axis=0, concat_axis=0, tiled=True)


def params(mib):
    return pltpu.CompilerParams(vmem_limit_bytes=mib << 20)


def cost(flops, nbytes, part=1):
    return pl.CostEstimate(flops=flops // part, bytes_accessed=nbytes // part, transcendentals=0)


def pack_kernel(slots, *refs):
    out = refs[-1]
    txt, img = refs[:slots], refs[slots : 2 * slots]
    heads = out.shape[0]
    t = txt[0].shape[0]
    for j in range(slots):
        lanes = slice(j * HEAD_SIZE, (j + 1) * HEAD_SIZE)
        for h in range(heads):
            cols = slice(h * HEAD_SIZE, (h + 1) * HEAD_SIZE)
            out[h, :t, lanes] = txt[j][:, cols]
            out[h, t:, lanes] = img[j][:, cols]


def pack_heads(txt, img, first, slots, heads, step=8):
    t, i = txt.shape[0], img.shape[0]
    per = heads // step

    def spec(rows, j):
        return pl.BlockSpec((rows, step * HEAD_SIZE), lambda g: (0, (first + j) * per + g))

    nbytes = 2 * (t + i) * slots * heads * HEAD_SIZE * 2
    return pl.pallas_call(
        functools.partial(pack_kernel, slots),
        grid=(per,),
        in_specs=[spec(t, j) for j in range(slots)] + [spec(i, j) for j in range(slots)],
        out_specs=pl.BlockSpec((step, t + i, slots * HEAD_SIZE), lambda g: (g, 0, 0)),
        out_shape=jax.ShapeDtypeStruct((heads, t + i, slots * HEAD_SIZE), BF16),
        compiler_params=params(56),
        cost_estimate=cost(0, nbytes),
    )(*([txt] * slots), *([img] * slots))


def d_image_kernel(cot, gate, adv, y, attn, out, here, ahead, behind, across):
    weighted = adv[0, 0] * gate[...]
    out[...] = (weighted * cot[...].astype(F32)).astype(BF16)
    width = here.shape[1]
    rows = attn.shape[1]
    count = out.shape[1] // width

    def part(hop):
        start = lax.rem(y[0, 0] + hop, count) * width
        return out[:, pl.ds(pl.multiple_of(start, width), width)]

    here[...] = part(0)
    for hop, ref in ((1, ahead), (count - 1, behind), (2, across)):
        ref[:, :rows] = attn[...]
        ref[:, rows:] = part(hop)


def d_image_call(cot, gate, adv, y, attn, count):
    rows, width = cot.shape
    part = width // count
    vmem = pl.BlockSpec(memory_space=pltpu.VMEM)
    smem = pl.BlockSpec(memory_space=pltpu.SMEM)
    return pl.pallas_call(
        d_image_kernel,
        in_specs=[vmem, vmem, smem, smem, vmem],
        out_specs=[vmem] * 5,
        out_shape=[jax.ShapeDtypeStruct((rows, width), BF16), jax.ShapeDtypeStruct((rows, part), BF16)]
        + [jax.ShapeDtypeStruct((rows, attn.shape[1] + part), BF16)] * 3,
        compiler_params=params(48),
        cost_estimate=cost(2 * rows * width, 6 * rows * width),
    )(cot, gate, adv, y, attn)


def partial_kernel(c, attn, here, m1, m2, m3, keep, low, high):
    block, half = keep.shape
    rows = m1.shape[1] - 2 * half
    at = pl.ds(pl.multiple_of(pl.program_id(0) * block, block), block)
    merged = (m1, m2, m3)
    value = lax.dot_general(
        jnp.concatenate([attn[...]] + [ref[:, at] for ref in merged], axis=0),
        jnp.concatenate([here[...]] + [ref[:, rows:] for ref in merged], axis=0),
        (((0,), (0,)), ((), ())),
        preferred_element_type=F32,
    )
    left, right = value[:, :half], value[:, half:]
    first = c[0, 0] == 0
    keep[...] = jnp.where(first, left, right).astype(BF16)
    send = jnp.where(first, right, left).astype(BF16)
    early = pl.program_id(0) < pl.num_programs(0) // 2

    @pl.when(early)
    def _():
        low[...] = send

    @pl.when(jnp.logical_not(early))
    def _():
        high[...] = send


def partial_call(c, attn, here, merged):
    tokens, rows = attn.shape
    cols = here.shape[1]
    block = 512
    half = rows // block // 2
    out = (block, cols // 2)
    return pl.pallas_call(
        partial_kernel,
        grid=(rows // block,),
        in_specs=[
            pl.BlockSpec(memory_space=pltpu.SMEM),
            pl.BlockSpec((tokens, block), lambda i: (0, i)),
            pl.BlockSpec((tokens, cols), lambda i: (0, 0)),
        ]
        + [pl.BlockSpec((tokens, rows + cols), lambda i: (0, 0))] * 3,
        out_specs=[
            pl.BlockSpec(out, lambda i: (i, 0)),
            pl.BlockSpec(out, lambda i: (jnp.minimum(i, half - 1), 0)),
            pl.BlockSpec(out, lambda i: (jnp.maximum(i - half, 0), 0)),
        ],
        out_shape=[
            jax.ShapeDtypeStruct((rows, cols // 2), BF16),
            jax.ShapeDtypeStruct((rows // 2, cols // 2), BF16),
            jax.ShapeDtypeStruct((rows // 2, cols // 2), BF16),
        ],
        compiler_params=params(40),
        cost_estimate=cost(8 * tokens * rows * cols, 8 * tokens * (rows + cols) + 2 * rows * cols, SMALL),
    )(c, attn, here, *merged)


def place_kernel(ring, keep, low, high, out):
    places, rows, _ = out.shape
    got = jnp.where(pl.program_id(0) == 0, low[...], high[...])
    value = (keep[...].astype(F32) + got.astype(F32)).astype(BF16)
    rows //= ring
    for y in range(ring):
        for place in range(places):
            at = (y * places + place) * rows
            out[place, y * rows : (y + 1) * rows] = value[at : at + rows]


def place_call(keep, got, ring, places, rows):
    cols = keep.shape[1]
    block = pl.BlockSpec((ring * places * rows, cols), lambda h: (h, 0))
    return pl.pallas_call(
        functools.partial(place_kernel, ring),
        grid=(len(got),),
        in_specs=[block] + [pl.BlockSpec((ring * places * rows, cols), lambda h: (0, 0))] * len(got),
        out_specs=pl.BlockSpec((places, ring * rows, cols), lambda h: (h, 0, 0)),
        out_shape=jax.ShapeDtypeStruct((len(got) * places, ring * rows, cols), BF16),
        compiler_params=params(40),
        cost_estimate=cost(0, 6 * keep.size, SMALL),
    )(keep, *got)


def ring_kernel(y, *refs):
    out = refs[-1]
    count = len(refs) - 1
    width = refs[0].shape[1]
    for hop in range(count):
        start = lax.rem(y[0, 0] + count - hop, count) * width
        out[:, pl.ds(pl.multiple_of(start, width), width)] = refs[hop][...]


def ring_call(y, pieces):
    rows, width = pieces[0].shape
    vmem = pl.BlockSpec(memory_space=pltpu.VMEM)
    return pl.pallas_call(
        ring_kernel,
        in_specs=[pl.BlockSpec(memory_space=pltpu.SMEM)] + [vmem] * len(pieces),
        out_specs=vmem,
        out_shape=jax.ShapeDtypeStruct((rows, width * len(pieces)), F32),
        compiler_params=params(16),
        cost_estimate=cost(0, 8 * rows * width * len(pieces), SMALL),
    )(y, *pieces)


def d_out_kernel(dimg, weight, cot_txt, adv, vt, vi, out):
    heads = out.shape[0]
    t = cot_txt.shape[0]
    total = lax.dot_general(dimg[...], weight[...], (((1,), (1,)), ((), ())), preferred_element_type=F32)
    total = total.astype(BF16)
    text = (adv[0, 0] * cot_txt[...].astype(F32)).astype(BF16)
    for h in range(heads):
        cols = slice(h * HEAD_SIZE, (h + 1) * HEAD_SIZE)
        out[h, :t, :HEAD_SIZE] = vt[:, cols]
        out[h, t:, :HEAD_SIZE] = vi[:, cols]
        out[h, :t, HEAD_SIZE:] = text[:, cols]
        out[h, t:, HEAD_SIZE:] = total[:, cols]


def d_out_call(dimg, weight, cot_txt, adv, txt, img, heads, step=4):
    rows, model = dimg.shape
    t = cot_txt.shape[0]
    width = step * HEAD_SIZE
    per = heads // step
    return pl.pallas_call(
        d_out_kernel,
        grid=(per,),
        in_specs=[
            pl.BlockSpec((rows, model), lambda g: (0, 0)),
            pl.BlockSpec((width, model), lambda g: (g, 0)),
            pl.BlockSpec((t, width), lambda g: (0, g)),
            pl.BlockSpec(memory_space=pltpu.SMEM),
            pl.BlockSpec((t, width), lambda g: (0, 2 * per + g)),
            pl.BlockSpec((rows, width), lambda g: (0, 2 * per + g)),
        ],
        out_specs=pl.BlockSpec((step, t + rows, 2 * HEAD_SIZE), lambda g: (g, 0, 0)),
        out_shape=jax.ShapeDtypeStruct((heads, t + rows, 2 * HEAD_SIZE), BF16),
        compiler_params=params(51),
        cost_estimate=cost(
            2 * rows * weight.size, 2 * (weight.size + dimg.size + 3 * (t + rows) * heads * HEAD_SIZE)
        ),
    )(dimg, weight, cot_txt, adv, txt, img)


def fold(array, combine):
    return combine(array.reshape(-1, 8, array.shape[1]), axis=0)


def exps_kernel(q, k, e_out, inv_out):
    chunks = [slice(at, at + CHUNK) for at in range(0, k.shape[0], CHUNK)]

    def scores(rows):
        return lax.dot_general(k[rows], q[...], (((1,), (1,)), ((), ())), preferred_element_type=F32)

    def fill(top):
        total = jnp.zeros((8, top.shape[1]), F32)
        top = top * (SCALE * LOG2E)
        for rows in chunks:
            low = jnp.exp2(scores(rows) * (SCALE * LOG2E) - top).astype(BF16)
            e_out[rows] = low
            total += fold(low.astype(F32), jnp.sum)
        total = jnp.sum(total, axis=0, keepdims=True)
        inv_out[...] = jnp.transpose(jnp.broadcast_to(1.0 / total, (HEAD_SIZE, total.shape[1])))
        return total

    total = fill(jnp.max(scores(chunks[0]), axis=0, keepdims=True))

    @pl.when(jnp.logical_not(jnp.max(total) < SAFE))
    def _():
        top = None
        for rows in chunks:
            part = fold(scores(rows), jnp.max)
            top = part if top is None else jnp.maximum(top, part)
        fill(jnp.max(top, axis=0, keepdims=True))


def exps_call(qk):
    n = qk.shape[0]
    block = BLOCK
    return pl.pallas_call(
        exps_kernel,
        grid=(n // block,),
        in_specs=[
            pl.BlockSpec((block, HEAD_SIZE), lambda i: (i, 0)),
            pl.BlockSpec((n, HEAD_SIZE), lambda i: (0, 1)),
        ],
        out_specs=[
            pl.BlockSpec((n, block), lambda i: (0, i)),
            pl.BlockSpec((block, HEAD_SIZE), lambda i: (i, 0)),
        ],
        out_shape=[
            jax.ShapeDtypeStruct((n, n), BF16),
            jax.ShapeDtypeStruct((n, HEAD_SIZE), F32),
        ],
        compiler_params=params(56),
        cost_estimate=cost(2 * n * n * HEAD_SIZE * 2, 2 * n * n, SMALL),
    )(qk, qk)


def grads_kernel(e, inv, q, k, v, d, out, dk, dv, prob_grads):
    step = pl.program_id(0)
    chunks = [slice(at, at + CHUNK) for at in range(0, k.shape[0], CHUNK)]

    @pl.when(step == 0)
    def _():
        dk[...] = jnp.zeros_like(dk)
        dv[...] = jnp.zeros_like(dv)

    inverse = inv[...]
    d_low = (d[...].astype(F32) * inverse).astype(BF16)
    centre = jnp.zeros((8, BLOCK), F32)
    for rows in chunks:
        probs = e[rows]
        part = lax.dot_general(v[rows], d_low, (((1,), (1,)), ((), ())), preferred_element_type=F32)
        prob_grads[rows] = part
        centre += fold(probs.astype(F32) * part, jnp.sum)
        dv[rows] += jnp.dot(probs, d_low, preferred_element_type=F32)
    centre = jnp.sum(centre, axis=0, keepdims=True) * jnp.transpose(inverse)[:1]
    dq = jnp.zeros((BLOCK, HEAD_SIZE), F32)
    for rows in chunks:
        score_grad = (e[rows].astype(F32) * (prob_grads[rows] - centre)).astype(BF16)
        dk[rows] += jnp.dot(score_grad, q[...], preferred_element_type=F32)
        dq += lax.dot_general(score_grad, k[rows], (((0,), (0,)), ((), ())), preferred_element_type=F32)
    out[pl.ds(pl.multiple_of(step * BLOCK, BLOCK), BLOCK), :HEAD_SIZE] = (dq * SCALE).astype(BF16)

    @pl.when(step == pl.num_programs(0) - 1)
    def _():
        out[:, HEAD_SIZE : 2 * HEAD_SIZE] = (dk[...] * SCALE).astype(BF16)
        out[:, 2 * HEAD_SIZE :] = dv[...].astype(BF16)


def grads_call(exps, inverse, qk, vd):
    n = qk.shape[0]
    block = lambda col: pl.BlockSpec((BLOCK, HEAD_SIZE), lambda i: (i, col))
    whole = lambda col: pl.BlockSpec((n, HEAD_SIZE), lambda i: (0, col))
    return pl.pallas_call(
        grads_kernel,
        grid=(n // BLOCK,),
        in_specs=[pl.BlockSpec((n, BLOCK), lambda i: (0, i)), block(0), block(0), whole(1), whole(0), block(1)],
        out_specs=pl.BlockSpec((n, 3 * HEAD_SIZE), lambda i: (0, 0)),
        out_shape=jax.ShapeDtypeStruct((n, 3 * HEAD_SIZE), BF16),
        scratch_shapes=[pltpu.VMEM((n, HEAD_SIZE), F32)] * 2 + [pltpu.VMEM((n, BLOCK), F32)],
        compiler_params=params(56),
        cost_estimate=cost(2 * n * n * HEAD_SIZE * 8, 2 * n * n, SMALL),
    )(exps, inverse, qk, qk, vd, vd)


def unpack_kernel(back, txt, img):
    t = txt.shape[0]
    for h in range(back.shape[0]):
        cols = slice(h * HEAD_SIZE, (h + 1) * HEAD_SIZE)
        txt[:, cols] = back[h, :t]
        img[:, cols] = back[h, t:]


def unpack_call(back, t):
    heads, tokens, _ = back.shape
    width = heads * HEAD_SIZE
    i = tokens - t
    return pl.pallas_call(
        unpack_kernel,
        grid=(3,),
        in_specs=[pl.BlockSpec((heads, tokens, HEAD_SIZE), lambda j: (0, 0, j))],
        out_specs=[
            pl.BlockSpec((t, width), lambda j: (0, j)),
            pl.BlockSpec((i, width), lambda j: (0, j)),
        ],
        out_shape=[
            jax.ShapeDtypeStruct((t, 3 * width), BF16),
            jax.ShapeDtypeStruct((i, 3 * width), BF16),
        ],
        compiler_params=params(24),
        cost_estimate=cost(0, 12 * tokens * width, SMALL),
    )(back)


def per_device(qkv_txt, qkv_img, attn_img, cot_txt, cot_img, gate, advantage, proj_weight):
    txt, img = qkv_txt[0], qkv_img[0]
    tokens = txt.shape[0] + img.shape[0]
    width = attn_img.shape[2]
    heads = width // HEAD_SIZE
    model = cot_img.shape[2]
    adv = advantage[:, None]
    index = lambda axes: lax.axis_index(axes).astype(jnp.int32).reshape(1, 1)
    y, core = index("y"), index("c")

    def shift(arrays, axes):
        perms = [[(i, (i + hop) % RING) for i in range(RING)] for hop in HOPS]
        return [lax.ppermute(array, axes, perm) for array, perm in zip(arrays, perms)]

    def swap(array):
        return lax.ppermute(array, "c", [(0, 1), (1, 0)])

    attn = attn_img[0]
    packed = pack_heads(txt, img, 0, 2, heads)
    qk = exchange(packed, SEQ)
    cot, attn, packed = lax.optimization_barrier((cot_img[0], attn, packed))
    d_image, here, *merged = d_image_call(cot, gate, adv, y, attn, RING)
    merged = shift(merged, "y")
    vd = d_out_call(d_image, proj_weight, cot_txt[0], adv, txt, img, heads)
    vd, qk = lax.optimization_barrier((vd, qk))
    vd = exchange(vd, SEQ)

    n = heads * tokens
    qk = qk.reshape(n, 2 * HEAD_SIZE)
    exps, inverse = exps_call(qk)
    attn, here, merged, inverse = lax.optimization_barrier((attn, here, merged, inverse))
    keep, low, high = partial_call(core, attn, here, merged)
    low, high = swap(low), swap(high)

    devices = lax.axis_size(ALL)
    rows = width // devices
    cols = keep.shape[1]
    product = place_call(keep, [low, high], RING, lax.axis_size(PLANE) // 2, 2 * rows)
    product = exchange(product, PLANE)

    vd = vd.reshape(n, 2 * HEAD_SIZE)
    grads = grads_call(exps, inverse, qk, vd).reshape(heads, tokens, 3 * HEAD_SIZE)
    grads, product = lax.optimization_barrier((grads, product))
    back = exchange(grads, SEQ)

    total = jnp.sum(product.astype(F32), axis=0) * (1.0 / (img.shape[0] * devices))
    total = total.reshape(RING, 2, rows, cols)
    c, y = core[0, 0], y[0, 0]
    own = lax.dynamic_index_in_dim(total, c, 1, keepdims=False)
    other = swap(lax.dynamic_index_in_dim(total, 1 - c, 1, keepdims=False))
    wide = jnp.where(c == 0, jnp.concatenate([own, other], -1), jnp.concatenate([other, own], -1))
    pick = lambda hop: lax.dynamic_index_in_dim(wide, (y + hop) % RING, 0, keepdims=False)
    behind, ahead, across = shift([pick(hop) for hop in HOPS], "y")
    grad_proj = ring_call(y.reshape(1, 1), [pick(0), behind, across, ahead])
    back, grad_proj = lax.optimization_barrier((back, grad_proj))

    dqkv_txt, dqkv_img = unpack_call(back, txt.shape[0])
    return (dqkv_txt[None], dqkv_img[None], grad_proj)


def solution(mesh):
    fine = Mesh(mesh.devices.reshape(2, 4, 2, 4, 2), ALL)
    dp = ("zh", "y")
    tokens = P(dp, SEQ, None)
    return jax.shard_map(
        per_device,
        mesh=fine,
        in_specs=(tokens, tokens, tokens, tokens, tokens, P(dp, None), P(dp), P()),
        out_specs=(tokens, tokens, P(dp + SEQ, None)),
        check_vma=False,
    )
```

```python
import functools

import jax
import jax.numpy as jnp
from jax import lax
from jax.experimental import pallas as pl
from jax.experimental.pallas import tpu as pltpu
from jax.sharding import Mesh, PartitionSpec as P

HEAD_SIZE = 128
SCALE = HEAD_SIZE ** (-0.5)
LOG2E = 1.4426950408889634
BLOCK = 512
CHUNK = 256
SMALL = 1000
SAFE = 2.0**40
SEQ = ("zl", "x", "c")
ALL = ("zh", "y", "zl", "x", "c")
PLANE = ("zh", "zl", "x")
RING = 4
HOPS = (1, RING - 1, 2)
SPAN = 256
BF16 = jnp.bfloat16
F32 = jnp.float32


def exchange(array, axes):
    return lax.all_to_all(array, axes, split_axis=0, concat_axis=0, tiled=True)


def params(mib):
    return pltpu.CompilerParams(vmem_limit_bytes=mib << 20)


def cost(flops, nbytes, part=1):
    return pl.CostEstimate(flops=flops // part, bytes_accessed=nbytes // part, transcendentals=0)


def pack_kernel(slots, *refs):
    out = refs[-1]
    txt, img = refs[:slots], refs[slots : 2 * slots]
    heads = out.shape[0]
    t = txt[0].shape[0]
    for j in range(slots):
        lanes = slice(j * HEAD_SIZE, (j + 1) * HEAD_SIZE)
        for h in range(heads):
            cols = slice(h * HEAD_SIZE, (h + 1) * HEAD_SIZE)
            out[h, :t, lanes] = txt[j][:, cols]
            out[h, t:, lanes] = img[j][:, cols]


def pack_heads(txt, img, first, slots, heads, step=8):
    t, i = txt.shape[0], img.shape[0]
    per = heads // step

    def spec(rows, j):
        return pl.BlockSpec((rows, step * HEAD_SIZE), lambda g: (0, (first + j) * per + g))

    nbytes = 2 * (t + i) * slots * heads * HEAD_SIZE * 2
    return pl.pallas_call(
        functools.partial(pack_kernel, slots),
        grid=(per,),
        in_specs=[spec(t, j) for j in range(slots)] + [spec(i, j) for j in range(slots)],
        out_specs=pl.BlockSpec((step, t + i, slots * HEAD_SIZE), lambda g: (g, 0, 0)),
        out_shape=jax.ShapeDtypeStruct((heads, t + i, slots * HEAD_SIZE), BF16),
        compiler_params=params(56),
        cost_estimate=cost(0, nbytes),
    )(*([txt] * slots), *([img] * slots))


def d_image_kernel(cot, gate, adv, y, attn, out, here, ahead, behind, across):
    weighted = adv[0, 0] * gate[...]
    out[...] = (weighted * cot[...].astype(F32)).astype(BF16)
    rows, cols = attn.shape[1] // 2, out.shape[1] // 2
    for hop, ref in zip((0,) + HOPS, (here, ahead, behind, across)):
        place = lax.rem(y[0, 0] + hop, RING)
        odd, upper = lax.rem(place, 2), lax.div(place, 2)
        for block in range(rows // SPAN):
            start = (2 * block + odd) * SPAN
            ref[:, block * SPAN : (block + 1) * SPAN] = attn[:, pl.ds(pl.multiple_of(start, SPAN), SPAN)]
        ref[:, rows:] = out[:, pl.ds(pl.multiple_of(upper * cols, cols), cols)]


def d_image_call(cot, gate, adv, y, attn):
    rows, width = cot.shape
    vmem = pl.BlockSpec(memory_space=pltpu.VMEM)
    smem = pl.BlockSpec(memory_space=pltpu.SMEM)
    payload = jax.ShapeDtypeStruct((rows, attn.shape[1] // 2 + width // 2), BF16)
    return pl.pallas_call(
        d_image_kernel,
        in_specs=[vmem, vmem, smem, smem, vmem],
        out_specs=[vmem] * 5,
        out_shape=[jax.ShapeDtypeStruct((rows, width), BF16)] + [payload] * 4,
        compiler_params=params(48),
        cost_estimate=cost(2 * rows * width, 6 * rows * width),
    )(cot, gate, adv, y, attn)


def partial_kernel(c, m0, m1, m2, m3, keep, low, high):
    block, half = keep.shape
    rows = m0.shape[1] - 2 * half
    at = pl.ds(pl.multiple_of(pl.program_id(0) * block, block), block)
    merged = (m0, m1, m2, m3)
    value = lax.dot_general(
        jnp.concatenate([ref[:, at] for ref in merged], axis=0),
        jnp.concatenate([ref[:, rows:] for ref in merged], axis=0),
        (((0,), (0,)), ((), ())),
        preferred_element_type=F32,
    )
    left, right = value[:, :half], value[:, half:]
    first = c[0, 0] == 0
    keep[...] = jnp.where(first, left, right).astype(BF16)
    send = jnp.where(first, right, left).astype(BF16)
    early = pl.program_id(0) < pl.num_programs(0) // 2

    @pl.when(early)
    def _():
        low[...] = send

    @pl.when(jnp.logical_not(early))
    def _():
        high[...] = send


def partial_call(c, merged, rows, cols):
    tokens = merged[0].shape[0]
    block = SPAN
    half = rows // block // 2
    out = (block, cols // 2)
    return pl.pallas_call(
        partial_kernel,
        grid=(rows // block,),
        in_specs=[pl.BlockSpec(memory_space=pltpu.SMEM)]
        + [pl.BlockSpec((tokens, rows + cols), lambda i: (0, 0))] * len(merged),
        out_specs=[
            pl.BlockSpec(out, lambda i: (i, 0)),
            pl.BlockSpec(out, lambda i: (jnp.minimum(i, half - 1), 0)),
            pl.BlockSpec(out, lambda i: (jnp.maximum(i - half, 0), 0)),
        ],
        out_shape=[
            jax.ShapeDtypeStruct((rows, cols // 2), BF16),
            jax.ShapeDtypeStruct((rows // 2, cols // 2), BF16),
            jax.ShapeDtypeStruct((rows // 2, cols // 2), BF16),
        ],
        compiler_params=params(40),
        cost_estimate=cost(8 * tokens * rows * cols, 8 * tokens * (rows + cols) + 2 * rows * cols, SMALL),
    )(c, *merged)


def place_kernel(ring, keep, low, high, out):
    places, rows, _ = out.shape
    got = jnp.where(pl.program_id(0) == 0, low[...], high[...])
    value = (keep[...].astype(F32) + got.astype(F32)).astype(BF16)
    rows //= ring
    for y in range(ring):
        for place in range(places):
            at = (y * places + place) * rows
            out[place, y * rows : (y + 1) * rows] = value[at : at + rows]


def place_call(keep, got, ring, places, rows):
    cols = keep.shape[1]
    block = pl.BlockSpec((ring * places * rows, cols), lambda h: (h, 0))
    return pl.pallas_call(
        functools.partial(place_kernel, ring),
        grid=(len(got),),
        in_specs=[block] + [pl.BlockSpec((ring * places * rows, cols), lambda h: (0, 0))] * len(got),
        out_specs=pl.BlockSpec((places, ring * rows, cols), lambda h: (h, 0, 0)),
        out_shape=jax.ShapeDtypeStruct((len(got) * places, ring * rows, cols), BF16),
        compiler_params=params(40),
        cost_estimate=cost(0, 6 * keep.size, SMALL),
    )(keep, *got)


def d_out_kernel(dimg, weight, cot_txt, adv, vt, vi, out):
    heads = out.shape[0]
    t = cot_txt.shape[0]
    total = lax.dot_general(dimg[...], weight[...], (((1,), (1,)), ((), ())), preferred_element_type=F32)
    total = total.astype(BF16)
    text = (adv[0, 0] * cot_txt[...].astype(F32)).astype(BF16)
    for h in range(heads):
        cols = slice(h * HEAD_SIZE, (h + 1) * HEAD_SIZE)
        out[h, :t, :HEAD_SIZE] = vt[:, cols]
        out[h, t:, :HEAD_SIZE] = vi[:, cols]
        out[h, :t, HEAD_SIZE:] = text[:, cols]
        out[h, t:, HEAD_SIZE:] = total[:, cols]


def d_out_call(dimg, weight, cot_txt, adv, txt, img, heads, step=4):
    rows, model = dimg.shape
    t = cot_txt.shape[0]
    width = step * HEAD_SIZE
    per = heads // step
    return pl.pallas_call(
        d_out_kernel,
        grid=(per,),
        in_specs=[
            pl.BlockSpec((rows, model), lambda g: (0, 0)),
            pl.BlockSpec((width, model), lambda g: (g, 0)),
            pl.BlockSpec((t, width), lambda g: (0, g)),
            pl.BlockSpec(memory_space=pltpu.SMEM),
            pl.BlockSpec((t, width), lambda g: (0, 2 * per + g)),
            pl.BlockSpec((rows, width), lambda g: (0, 2 * per + g)),
        ],
        out_specs=pl.BlockSpec((step, t + rows, 2 * HEAD_SIZE), lambda g: (g, 0, 0)),
        out_shape=jax.ShapeDtypeStruct((heads, t + rows, 2 * HEAD_SIZE), BF16),
        compiler_params=params(51),
        cost_estimate=cost(
            2 * rows * weight.size, 2 * (weight.size + dimg.size + 3 * (t + rows) * heads * HEAD_SIZE)
        ),
    )(dimg, weight, cot_txt, adv, txt, img)


def fold(array, combine):
    return combine(array.reshape(-1, 8, array.shape[1]), axis=0)


def exps_kernel(q, k, e_out, inv_out):
    chunks = [slice(at, at + CHUNK) for at in range(0, k.shape[0], CHUNK)]

    def scores(rows):
        return lax.dot_general(k[rows], q[...], (((1,), (1,)), ((), ())), preferred_element_type=F32)

    def fill(top):
        total = jnp.zeros((8, top.shape[1]), F32)
        top = top * (SCALE * LOG2E)
        for rows in chunks:
            low = jnp.exp2(scores(rows) * (SCALE * LOG2E) - top).astype(BF16)
            e_out[rows] = low
            total += fold(low.astype(F32), jnp.sum)
        total = jnp.sum(total, axis=0, keepdims=True)
        inv_out[...] = jnp.transpose(jnp.broadcast_to(1.0 / total, (HEAD_SIZE, total.shape[1])))
        return total

    total = fill(jnp.max(scores(chunks[0]), axis=0, keepdims=True))

    @pl.when(jnp.logical_not(jnp.max(total) < SAFE))
    def _():
        top = None
        for rows in chunks:
            part = fold(scores(rows), jnp.max)
            top = part if top is None else jnp.maximum(top, part)
        fill(jnp.max(top, axis=0, keepdims=True))


def exps_call(qk):
    n = qk.shape[0]
    block = BLOCK
    return pl.pallas_call(
        exps_kernel,
        grid=(n // block,),
        in_specs=[
            pl.BlockSpec((block, HEAD_SIZE), lambda i: (i, 0)),
            pl.BlockSpec((n, HEAD_SIZE), lambda i: (0, 1)),
        ],
        out_specs=[
            pl.BlockSpec((n, block), lambda i: (0, i)),
            pl.BlockSpec((block, HEAD_SIZE), lambda i: (i, 0)),
        ],
        out_shape=[
            jax.ShapeDtypeStruct((n, n), BF16),
            jax.ShapeDtypeStruct((n, HEAD_SIZE), F32),
        ],
        compiler_params=params(56),
        cost_estimate=cost(2 * n * n * HEAD_SIZE * 2, 2 * n * n, SMALL),
    )(qk, qk)


def grads_kernel(e, inv, q, k, v, d, out, dk, dv, prob_grads):
    step = pl.program_id(0)
    chunks = [slice(at, at + CHUNK) for at in range(0, k.shape[0], CHUNK)]

    @pl.when(step == 0)
    def _():
        dk[...] = jnp.zeros_like(dk)
        dv[...] = jnp.zeros_like(dv)

    inverse = inv[...]
    d_low = (d[...].astype(F32) * inverse).astype(BF16)
    centre = jnp.zeros((8, BLOCK), F32)
    for rows in chunks:
        probs = e[rows]
        part = lax.dot_general(v[rows], d_low, (((1,), (1,)), ((), ())), preferred_element_type=F32)
        prob_grads[rows] = part
        centre += fold(probs.astype(F32) * part, jnp.sum)
        dv[rows] += jnp.dot(probs, d_low, preferred_element_type=F32)
    centre = jnp.sum(centre, axis=0, keepdims=True) * jnp.transpose(inverse)[:1]
    dq = jnp.zeros((BLOCK, HEAD_SIZE), F32)
    for rows in chunks:
        score_grad = (e[rows].astype(F32) * (prob_grads[rows] - centre)).astype(BF16)
        dk[rows] += jnp.dot(score_grad, q[...], preferred_element_type=F32)
        dq += lax.dot_general(score_grad, k[rows], (((0,), (0,)), ((), ())), preferred_element_type=F32)
    out[pl.ds(pl.multiple_of(step * BLOCK, BLOCK), BLOCK), :HEAD_SIZE] = (dq * SCALE).astype(BF16)

    @pl.when(step == pl.num_programs(0) - 1)
    def _():
        out[:, HEAD_SIZE : 2 * HEAD_SIZE] = (dk[...] * SCALE).astype(BF16)
        out[:, 2 * HEAD_SIZE :] = dv[...].astype(BF16)


def grads_call(exps, inverse, qk, vd):
    n = qk.shape[0]
    block = lambda col: pl.BlockSpec((BLOCK, HEAD_SIZE), lambda i: (i, col))
    whole = lambda col: pl.BlockSpec((n, HEAD_SIZE), lambda i: (0, col))
    return pl.pallas_call(
        grads_kernel,
        grid=(n // BLOCK,),
        in_specs=[pl.BlockSpec((n, BLOCK), lambda i: (0, i)), block(0), block(0), whole(1), whole(0), block(1)],
        out_specs=pl.BlockSpec((n, 3 * HEAD_SIZE), lambda i: (0, 0)),
        out_shape=jax.ShapeDtypeStruct((n, 3 * HEAD_SIZE), BF16),
        scratch_shapes=[pltpu.VMEM((n, HEAD_SIZE), F32)] * 2 + [pltpu.VMEM((n, BLOCK), F32)],
        compiler_params=params(56),
        cost_estimate=cost(2 * n * n * HEAD_SIZE * 8, 2 * n * n, SMALL),
    )(exps, inverse, qk, qk, vd, vd)


def unpack_kernel(back, txt, img):
    t = txt.shape[0]
    for h in range(back.shape[0]):
        cols = slice(h * HEAD_SIZE, (h + 1) * HEAD_SIZE)
        txt[:, cols] = back[h, :t]
        img[:, cols] = back[h, t:]


def unpack_call(back, t):
    heads, tokens, _ = back.shape
    width = heads * HEAD_SIZE
    i = tokens - t
    return pl.pallas_call(
        unpack_kernel,
        grid=(3,),
        in_specs=[pl.BlockSpec((heads, tokens, HEAD_SIZE), lambda j: (0, 0, j))],
        out_specs=[
            pl.BlockSpec((t, width), lambda j: (0, j)),
            pl.BlockSpec((i, width), lambda j: (0, j)),
        ],
        out_shape=[
            jax.ShapeDtypeStruct((t, 3 * width), BF16),
            jax.ShapeDtypeStruct((i, 3 * width), BF16),
        ],
        compiler_params=params(24),
        cost_estimate=cost(0, 12 * tokens * width, SMALL),
    )(back)


def per_device(qkv_txt, qkv_img, attn_img, cot_txt, cot_img, gate, advantage, proj_weight):
    txt, img = qkv_txt[0], qkv_img[0]
    tokens = txt.shape[0] + img.shape[0]
    width = attn_img.shape[2]
    heads = width // HEAD_SIZE
    model = cot_img.shape[2]
    adv = advantage[:, None]
    index = lambda axes: lax.axis_index(axes).astype(jnp.int32).reshape(1, 1)
    y, core = index("y"), index("c")

    def shift(arrays, axes):
        perms = [[(i, (i + hop) % RING) for i in range(RING)] for hop in HOPS]
        return [lax.ppermute(array, axes, perm) for array, perm in zip(arrays, perms)]

    def swap(array):
        return lax.ppermute(array, "c", [(0, 1), (1, 0)])

    attn = attn_img[0]
    packed = pack_heads(txt, img, 0, 2, heads)
    qk = exchange(packed, SEQ)
    cot, attn, packed = lax.optimization_barrier((cot_img[0], attn, packed))
    d_image, here, *merged = d_image_call(cot, gate, adv, y, attn)
    merged = [here, *shift(merged, "y")]
    vd = d_out_call(d_image, proj_weight, cot_txt[0], adv, txt, img, heads)
    vd, qk = lax.optimization_barrier((vd, qk))
    vd = exchange(vd, SEQ)

    n = heads * tokens
    qk = qk.reshape(n, 2 * HEAD_SIZE)
    exps, inverse = exps_call(qk)
    merged, inverse = lax.optimization_barrier((merged, inverse))
    keep, low, high = partial_call(core, merged, width // 2, model // 2)
    low, high = swap(low), swap(high)

    devices = lax.axis_size(ALL)
    rows = width // devices
    cols = keep.shape[1]
    product = place_call(keep, [low, high], RING // 2, lax.axis_size(PLANE) // 2, 2 * rows)
    product = exchange(product, PLANE)

    vd = vd.reshape(n, 2 * HEAD_SIZE)
    grads = grads_call(exps, inverse, qk, vd).reshape(heads, tokens, 3 * HEAD_SIZE)
    grads, product = lax.optimization_barrier((grads, product))
    back = exchange(grads, SEQ)

    total = jnp.sum(product.astype(F32), axis=0) * (1.0 / (img.shape[0] * devices))
    total = total.reshape(2, 2, rows, cols)
    c, upper = core[0, 0], y[0, 0] // 2

    def joined(first, own, other):
        return jnp.where(first, jnp.concatenate([own, other], -1), jnp.concatenate([other, own], -1))

    own = lax.dynamic_index_in_dim(total, c, 1, keepdims=False)
    other = swap(lax.dynamic_index_in_dim(total, 1 - c, 1, keepdims=False))
    wide = joined(c == 0, own, other)
    own = lax.dynamic_index_in_dim(wide, upper, 0, keepdims=False)
    other = lax.dynamic_index_in_dim(wide, 1 - upper, 0, keepdims=False)
    other = lax.ppermute(other, "y", [(i, (i + 2) % RING) for i in range(RING)])
    grad_proj = joined(upper == 0, own, other)
    back, grad_proj = lax.optimization_barrier((back, grad_proj))

    dqkv_txt, dqkv_img = unpack_call(back, txt.shape[0])
    return (dqkv_txt[None], dqkv_img[None], grad_proj)


def solution(mesh):
    fine = Mesh(mesh.devices.reshape(2, 4, 2, 4, 2), ALL)
    dp = ("zh", "y")
    tokens = P(dp, SEQ, None)
    return jax.shard_map(
        per_device,
        mesh=fine,
        in_specs=(tokens, tokens, tokens, tokens, tokens, P(dp, None), P(dp), P()),
        out_specs=(tokens, tokens, P(dp + SEQ, None)),
        check_vma=False,
    )
```

```python
import functools

import jax
import jax.numpy as jnp
from jax import lax
from jax.experimental import pallas as pl
from jax.experimental.pallas import tpu as pltpu
from jax.sharding import Mesh, PartitionSpec as P

HEAD_SIZE = 128
SCALE = HEAD_SIZE ** (-0.5)
LOG2E = 1.4426950408889634
BLOCK = 512
CHUNK = 256
SMALL = 1000
SAFE = 2.0**40
SEQ = ("zl", "x", "c")
ALL = ("zh", "y", "zl", "x", "c")
PLANE = ("zh", "zl", "x")
RING = 4
HOPS = (1, RING - 1, 2)
SPAN = 256
BF16 = jnp.bfloat16
F32 = jnp.float32


def exchange(array, axes):
    return lax.all_to_all(array, axes, split_axis=0, concat_axis=0, tiled=True)


def params(mib):
    return pltpu.CompilerParams(vmem_limit_bytes=mib << 20)


def cost(flops, nbytes, part=1):
    return pl.CostEstimate(flops=flops // part, bytes_accessed=nbytes // part, transcendentals=0)


def pack_kernel(slots, *refs):
    out = refs[-1]
    txt, img = refs[:slots], refs[slots : 2 * slots]
    heads = out.shape[0]
    t = txt[0].shape[0]
    for j in range(slots):
        lanes = slice(j * HEAD_SIZE, (j + 1) * HEAD_SIZE)
        for h in range(heads):
            cols = slice(h * HEAD_SIZE, (h + 1) * HEAD_SIZE)
            out[h, :t, lanes] = txt[j][:, cols]
            out[h, t:, lanes] = img[j][:, cols]


def pack_heads(txt, img, first, slots, heads, step=8):
    t, i = txt.shape[0], img.shape[0]
    per = heads // step

    def spec(rows, j):
        return pl.BlockSpec((rows, step * HEAD_SIZE), lambda g: (0, (first + j) * per + g))

    nbytes = 2 * (t + i) * slots * heads * HEAD_SIZE * 2
    return pl.pallas_call(
        functools.partial(pack_kernel, slots),
        grid=(per,),
        in_specs=[spec(t, j) for j in range(slots)] + [spec(i, j) for j in range(slots)],
        out_specs=pl.BlockSpec((step, t + i, slots * HEAD_SIZE), lambda g: (g, 0, 0)),
        out_shape=jax.ShapeDtypeStruct((heads, t + i, slots * HEAD_SIZE), BF16),
        compiler_params=params(56),
        cost_estimate=cost(0, nbytes),
    )(*([txt] * slots), *([img] * slots))


def d_image_kernel(cot, gate, adv, y, attn, out, here, ahead, behind, across):
    weighted = adv[0, 0] * gate[...]
    out[...] = (weighted * cot[...].astype(F32)).astype(BF16)
    rows, cols = attn.shape[1] // 2, out.shape[1] // 2
    for hop, ref in zip((0,) + HOPS, (here, ahead, behind, across)):
        place = lax.rem(y[0, 0] + hop, RING)
        odd, upper = lax.rem(place, 2), lax.div(place, 2)
        for block in range(rows // SPAN):
            start = (2 * block + odd) * SPAN
            ref[:, block * SPAN : (block + 1) * SPAN] = attn[:, pl.ds(pl.multiple_of(start, SPAN), SPAN)]
        ref[:, rows:] = out[:, pl.ds(pl.multiple_of(upper * cols, cols), cols)]


def d_image_call(cot, gate, adv, y, attn):
    rows, width = cot.shape
    vmem = pl.BlockSpec(memory_space=pltpu.VMEM)
    smem = pl.BlockSpec(memory_space=pltpu.SMEM)
    payload = jax.ShapeDtypeStruct((rows, attn.shape[1] // 2 + width // 2), BF16)
    return pl.pallas_call(
        d_image_kernel,
        in_specs=[vmem, vmem, smem, smem, vmem],
        out_specs=[vmem] * 5,
        out_shape=[jax.ShapeDtypeStruct((rows, width), BF16)] + [payload] * 4,
        compiler_params=params(48),
        cost_estimate=cost(2 * rows * width, 6 * rows * width),
    )(cot, gate, adv, y, attn)


def partial_kernel(c, m0, m1, m2, m3, keep, low, high):
    rows, half = keep.shape
    merged = (m0, m1, m2, m3)
    rhs = jnp.concatenate([ref[:, rows:] for ref in merged], axis=0)
    first = c[0, 0] == 0
    for start in range(0, rows, SPAN):
        lhs = jnp.concatenate([ref[:, start : start + SPAN] for ref in merged], axis=0)
        value = lax.dot_general(lhs, rhs, (((0,), (0,)), ((), ())), preferred_element_type=F32)
        left, right = value[:, :half], value[:, half:]
        keep[start : start + SPAN] = jnp.where(first, left, right).astype(BF16)
        out, skip = (low, 0) if start < rows // 2 else (high, rows // 2)
        out[start - skip : start - skip + SPAN] = jnp.where(first, right, left).astype(BF16)


def partial_call(c, merged, rows, cols):
    tokens = merged[0].shape[0]
    vmem = pl.BlockSpec(memory_space=pltpu.VMEM)
    return pl.pallas_call(
        partial_kernel,
        in_specs=[pl.BlockSpec(memory_space=pltpu.SMEM)] + [vmem] * len(merged),
        out_specs=[vmem] * 3,
        out_shape=[
            jax.ShapeDtypeStruct((rows, cols // 2), BF16),
            jax.ShapeDtypeStruct((rows // 2, cols // 2), BF16),
            jax.ShapeDtypeStruct((rows // 2, cols // 2), BF16),
        ],
        compiler_params=params(40),
        cost_estimate=cost(8 * tokens * rows * cols, 8 * tokens * (rows + cols) + 2 * rows * cols, SMALL),
    )(c, *merged)


def place_kernel(ring, keep, low, high, out, staged, sems):
    places, rows, _ = out.shape
    half = places // 2
    unit = rows // ring
    copies = []
    for part, got in enumerate((low, high)):
        for y in range(ring):
            for place in range(half):
                at = (y * half + place) * unit
                mine = keep[part * got.shape[0] + at : part * got.shape[0] + at + unit]
                value = mine.astype(F32) + got[at : at + unit].astype(F32)
                staged[part * half + place, y * unit : (y + 1) * unit] = value.astype(BF16)
        span = pl.ds(part * half, half)
        copies.append(pltpu.make_async_copy(staged.at[span], out.at[span], sems.at[part]))
        copies[-1].start()
    for copy in copies:
        copy.wait()


def place_call(keep, got, ring, places, rows):
    cols = keep.shape[1]
    shape = (len(got) * places, ring * rows, cols)
    vmem = pl.BlockSpec(memory_space=pltpu.VMEM)
    return pl.pallas_call(
        functools.partial(place_kernel, ring),
        in_specs=[vmem] * 3,
        out_specs=pl.BlockSpec(memory_space=pl.ANY),
        out_shape=jax.ShapeDtypeStruct(shape, BF16),
        scratch_shapes=[pltpu.VMEM(shape, BF16), pltpu.SemaphoreType.DMA((len(got),))],
        compiler_params=params(40),
        cost_estimate=cost(0, 6 * keep.size, SMALL),
    )(keep, *got)


def d_out_kernel(dimg, weight, cot_txt, adv, vt, vi, out):
    heads = out.shape[0]
    t = cot_txt.shape[0]
    total = lax.dot_general(dimg[...], weight[...], (((1,), (1,)), ((), ())), preferred_element_type=F32)
    total = total.astype(BF16)
    text = (adv[0, 0] * cot_txt[...].astype(F32)).astype(BF16)
    for h in range(heads):
        cols = slice(h * HEAD_SIZE, (h + 1) * HEAD_SIZE)
        out[h, :t, :HEAD_SIZE] = vt[:, cols]
        out[h, t:, :HEAD_SIZE] = vi[:, cols]
        out[h, :t, HEAD_SIZE:] = text[:, cols]
        out[h, t:, HEAD_SIZE:] = total[:, cols]


def d_out_call(dimg, weight, cot_txt, adv, txt, img, heads, step=8):
    rows, model = dimg.shape
    t = cot_txt.shape[0]
    width = step * HEAD_SIZE
    per = heads // step
    return pl.pallas_call(
        d_out_kernel,
        grid=(per,),
        in_specs=[
            pl.BlockSpec((rows, model), lambda g: (0, 0)),
            pl.BlockSpec((width, model), lambda g: (g, 0)),
            pl.BlockSpec((t, width), lambda g: (0, g)),
            pl.BlockSpec(memory_space=pltpu.SMEM),
            pl.BlockSpec((t, width), lambda g: (0, 2 * per + g)),
            pl.BlockSpec((rows, width), lambda g: (0, 2 * per + g)),
        ],
        out_specs=pl.BlockSpec((step, t + rows, 2 * HEAD_SIZE), lambda g: (g, 0, 0)),
        out_shape=jax.ShapeDtypeStruct((heads, t + rows, 2 * HEAD_SIZE), BF16),
        compiler_params=params(51),
        cost_estimate=cost(
            2 * rows * weight.size, 2 * (weight.size + dimg.size + 3 * (t + rows) * heads * HEAD_SIZE)
        ),
    )(dimg, weight, cot_txt, adv, txt, img)


def fold(array, combine):
    return combine(array.reshape(-1, 8, array.shape[1]), axis=0)


def exps_kernel(q, k, e_out, inv_out):
    chunks = [slice(at, at + CHUNK) for at in range(0, k.shape[0], CHUNK)]

    def scores(rows):
        return lax.dot_general(k[rows], q[...], (((1,), (1,)), ((), ())), preferred_element_type=F32)

    def fill(top):
        total = jnp.zeros((8, top.shape[1]), F32)
        top = top * (SCALE * LOG2E)
        for rows in chunks:
            low = jnp.exp2(scores(rows) * (SCALE * LOG2E) - top).astype(BF16)
            e_out[rows] = low
            total += fold(low.astype(F32), jnp.sum)
        total = jnp.sum(total, axis=0, keepdims=True)
        inv_out[...] = jnp.transpose(jnp.broadcast_to(1.0 / total, (HEAD_SIZE, total.shape[1])))
        return total

    total = fill(jnp.max(scores(chunks[0]), axis=0, keepdims=True))

    @pl.when(jnp.logical_not(jnp.max(total) < SAFE))
    def _():
        top = None
        for rows in chunks:
            part = fold(scores(rows), jnp.max)
            top = part if top is None else jnp.maximum(top, part)
        fill(jnp.max(top, axis=0, keepdims=True))


def exps_call(qk):
    n = qk.shape[0]
    block = BLOCK
    return pl.pallas_call(
        exps_kernel,
        grid=(n // block,),
        in_specs=[
            pl.BlockSpec((block, HEAD_SIZE), lambda i: (i, 0)),
            pl.BlockSpec((n, HEAD_SIZE), lambda i: (0, 1)),
        ],
        out_specs=[
            pl.BlockSpec((n, block), lambda i: (0, i)),
            pl.BlockSpec((block, HEAD_SIZE), lambda i: (i, 0)),
        ],
        out_shape=[
            jax.ShapeDtypeStruct((n, n), BF16),
            jax.ShapeDtypeStruct((n, HEAD_SIZE), F32),
        ],
        compiler_params=params(56),
        cost_estimate=cost(2 * n * n * HEAD_SIZE * 2, 2 * n * n, SMALL),
    )(qk, qk)


def grads_kernel(e, inv, q, k, v, d, out, dk, dv, prob_grads):
    step = pl.program_id(0)
    chunks = [slice(at, at + CHUNK) for at in range(0, k.shape[0], CHUNK)]

    @pl.when(step == 0)
    def _():
        dk[...] = jnp.zeros_like(dk)
        dv[...] = jnp.zeros_like(dv)

    inverse = inv[...]
    d_low = (d[...].astype(F32) * inverse).astype(BF16)
    centre = jnp.zeros((8, BLOCK), F32)
    for rows in chunks:
        probs = e[rows]
        part = lax.dot_general(v[rows], d_low, (((1,), (1,)), ((), ())), preferred_element_type=F32)
        prob_grads[rows] = part
        centre += fold(probs.astype(F32) * part, jnp.sum)
        dv[rows] += jnp.dot(probs, d_low, preferred_element_type=F32)
    centre = jnp.sum(centre, axis=0, keepdims=True) * jnp.transpose(inverse)[:1]
    dq = jnp.zeros((BLOCK, HEAD_SIZE), F32)
    for rows in chunks:
        score_grad = (e[rows].astype(F32) * (prob_grads[rows] - centre)).astype(BF16)
        dk[rows] += jnp.dot(score_grad, q[...], preferred_element_type=F32)
        dq += lax.dot_general(score_grad, k[rows], (((0,), (0,)), ((), ())), preferred_element_type=F32)
    out[pl.ds(pl.multiple_of(step * BLOCK, BLOCK), BLOCK), :HEAD_SIZE] = (dq * SCALE).astype(BF16)

    @pl.when(step == pl.num_programs(0) - 1)
    def _():
        out[:, HEAD_SIZE : 2 * HEAD_SIZE] = (dk[...] * SCALE).astype(BF16)
        out[:, 2 * HEAD_SIZE :] = dv[...].astype(BF16)


def grads_call(exps, inverse, qk, vd):
    n = qk.shape[0]
    block = lambda col: pl.BlockSpec((BLOCK, HEAD_SIZE), lambda i: (i, col))
    whole = lambda col: pl.BlockSpec((n, HEAD_SIZE), lambda i: (0, col))
    return pl.pallas_call(
        grads_kernel,
        grid=(n // BLOCK,),
        in_specs=[pl.BlockSpec((n, BLOCK), lambda i: (0, i)), block(0), block(0), whole(1), whole(0), block(1)],
        out_specs=pl.BlockSpec((n, 3 * HEAD_SIZE), lambda i: (0, 0)),
        out_shape=jax.ShapeDtypeStruct((n, 3 * HEAD_SIZE), BF16),
        scratch_shapes=[pltpu.VMEM((n, HEAD_SIZE), F32)] * 2 + [pltpu.VMEM((n, BLOCK), F32)],
        compiler_params=params(56),
        cost_estimate=cost(2 * n * n * HEAD_SIZE * 8, 2 * n * n, SMALL),
    )(exps, inverse, qk, qk, vd, vd)


def unpack_kernel(back, txt, img, txt_rows, img_rows, sems):
    heads, _, lanes = back.shape
    t = txt.shape[0]
    width = heads * HEAD_SIZE
    copies = []
    for slot in range(lanes // HEAD_SIZE):
        source = slice(slot * HEAD_SIZE, (slot + 1) * HEAD_SIZE)
        for h in range(heads):
            target = slice(slot * width + h * HEAD_SIZE, slot * width + (h + 1) * HEAD_SIZE)
            txt_rows[:, target] = back[h, :t, source]
            img_rows[:, target] = back[h, t:, source]
        whole = pl.ds(slot * width, width)
        for near, far in ((txt_rows, txt), (img_rows, img)):
            copy = pltpu.make_async_copy(near.at[:, whole], far.at[:, whole], sems.at[len(copies)])
            copy.start()
            copies.append(copy)
    for copy in copies:
        copy.wait()


def unpack_call(back, t):
    heads, tokens, lanes = back.shape
    shapes = [(t, heads * lanes), (tokens - t, heads * lanes)]
    return pl.pallas_call(
        unpack_kernel,
        in_specs=[pl.BlockSpec(memory_space=pltpu.VMEM)],
        out_specs=[pl.BlockSpec(memory_space=pl.ANY)] * 2,
        out_shape=[jax.ShapeDtypeStruct(shape, BF16) for shape in shapes],
        scratch_shapes=[pltpu.VMEM(shape, BF16) for shape in shapes]
        + [pltpu.SemaphoreType.DMA((2 * lanes // HEAD_SIZE,))],
        compiler_params=params(24),
        cost_estimate=cost(0, 2 * back.size, SMALL),
    )(back)


def per_device(qkv_txt, qkv_img, attn_img, cot_txt, cot_img, gate, advantage, proj_weight):
    txt, img = qkv_txt[0], qkv_img[0]
    tokens = txt.shape[0] + img.shape[0]
    width = attn_img.shape[2]
    heads = width // HEAD_SIZE
    model = cot_img.shape[2]
    adv = advantage[:, None]
    index = lambda axes: lax.axis_index(axes).astype(jnp.int32).reshape(1, 1)
    y, core = index("y"), index("c")

    def shift(arrays, axes):
        perms = [[(i, (i + hop) % RING) for i in range(RING)] for hop in HOPS]
        return [lax.ppermute(array, axes, perm) for array, perm in zip(arrays, perms)]

    def swap(array):
        return lax.ppermute(array, "c", [(0, 1), (1, 0)])

    attn = attn_img[0]
    packed = pack_heads(txt, img, 0, 2, heads)
    qk = exchange(packed, SEQ)
    cot, attn, packed = lax.optimization_barrier((cot_img[0], attn, packed))
    d_image, here, *merged = d_image_call(cot, gate, adv, y, attn)
    merged = [here, *shift(merged, "y")]
    vd = d_out_call(d_image, proj_weight, cot_txt[0], adv, txt, img, heads)
    vd, qk = lax.optimization_barrier((vd, qk))
    vd = exchange(vd, SEQ)

    n = heads * tokens
    qk = qk.reshape(n, 2 * HEAD_SIZE)
    exps, inverse = exps_call(qk)
    merged, inverse = lax.optimization_barrier((merged, inverse))
    keep, low, high = partial_call(core, merged, width // 2, model // 2)
    low, high = swap(low), swap(high)

    devices = lax.axis_size(ALL)
    rows = width // devices
    cols = keep.shape[1]
    product = place_call(keep, [low, high], RING // 2, lax.axis_size(PLANE) // 2, 2 * rows)
    product = exchange(product, PLANE)

    vd = vd.reshape(n, 2 * HEAD_SIZE)
    grads = grads_call(exps, inverse, qk, vd).reshape(heads, tokens, 3 * HEAD_SIZE)
    grads, product = lax.optimization_barrier((grads, product))
    back = exchange(grads, SEQ)

    total = jnp.sum(product.astype(F32), axis=0) * (1.0 / (img.shape[0] * devices))
    total = total.reshape(2, 2, rows, cols)
    c, upper = core[0, 0], y[0, 0] // 2

    def joined(first, own, other):
        return jnp.where(first, jnp.concatenate([own, other], -1), jnp.concatenate([other, own], -1))

    own = lax.dynamic_index_in_dim(total, c, 1, keepdims=False)
    other = swap(lax.dynamic_index_in_dim(total, 1 - c, 1, keepdims=False))
    wide = joined(c == 0, own, other)
    own = lax.dynamic_index_in_dim(wide, upper, 0, keepdims=False)
    other = lax.dynamic_index_in_dim(wide, 1 - upper, 0, keepdims=False)
    other = lax.ppermute(other, "y", [(i, (i + 2) % RING) for i in range(RING)])
    grad_proj = joined(upper == 0, own, other)
    back, grad_proj = lax.optimization_barrier((back, grad_proj))

    dqkv_txt, dqkv_img = unpack_call(back, txt.shape[0])
    return (dqkv_txt[None], dqkv_img[None], grad_proj)


def solution(mesh):
    fine = Mesh(mesh.devices.reshape(2, 4, 2, 4, 2), ALL)
    dp = ("zh", "y")
    tokens = P(dp, SEQ, None)
    return jax.shard_map(
        per_device,
        mesh=fine,
        in_specs=(tokens, tokens, tokens, tokens, tokens, P(dp, None), P(dp), P()),
        out_specs=(tokens, tokens, P(dp + SEQ, None)),
        check_vma=False,
    )
```

```python
import functools

import jax
import jax.numpy as jnp
from jax import lax
from jax.experimental import pallas as pl
from jax.experimental.pallas import tpu as pltpu
from jax.sharding import Mesh, PartitionSpec as P

HEAD_SIZE = 128
SCALE = HEAD_SIZE ** (-0.5)
LOG2E = 1.4426950408889634
BLOCK = 512
CHUNK = 256
SMALL = 1000
SAFE = 2.0**40
SEQ = ("zl", "x", "c")
ALL = ("zh", "y", "zl", "x", "c")
PLANE = ("zh", "zl", "x")
RING = 4
HOPS = (1, RING - 1, 2)
SPAN = 256
BF16 = jnp.bfloat16
F32 = jnp.float32


def exchange(array, axes):
    return lax.all_to_all(array, axes, split_axis=0, concat_axis=0, tiled=True)


def params(mib):
    return pltpu.CompilerParams(vmem_limit_bytes=mib << 20)


def cost(flops, nbytes, part=1):
    return pl.CostEstimate(flops=flops // part, bytes_accessed=nbytes // part, transcendentals=0)


def pack_kernel(slots, *refs):
    out = refs[-1]
    txt, img = refs[:slots], refs[slots : 2 * slots]
    heads = out.shape[0]
    t = txt[0].shape[0]
    for j in range(slots):
        lanes = slice(j * HEAD_SIZE, (j + 1) * HEAD_SIZE)
        for h in range(heads):
            cols = slice(h * HEAD_SIZE, (h + 1) * HEAD_SIZE)
            out[h, :t, lanes] = txt[j][:, cols]
            out[h, t:, lanes] = img[j][:, cols]


def pack_heads(txt, img, first, slots, heads, step=8):
    t, i = txt.shape[0], img.shape[0]
    per = heads // step

    def spec(rows, j):
        return pl.BlockSpec((rows, step * HEAD_SIZE), lambda g: (0, (first + j) * per + g))

    nbytes = 2 * (t + i) * slots * heads * HEAD_SIZE * 2
    return pl.pallas_call(
        functools.partial(pack_kernel, slots),
        grid=(per,),
        in_specs=[spec(t, j) for j in range(slots)] + [spec(i, j) for j in range(slots)],
        out_specs=pl.BlockSpec((step, t + i, slots * HEAD_SIZE), lambda g: (g, 0, 0)),
        out_shape=jax.ShapeDtypeStruct((heads, t + i, slots * HEAD_SIZE), BF16),
        compiler_params=params(56),
        cost_estimate=cost(0, nbytes),
    )(*([txt] * slots), *([img] * slots))


def d_image_kernel(cot, gate, adv, y, attn, out, here, ahead, behind, across):
    weighted = adv[0, 0] * gate[...]
    out[...] = (weighted * cot[...].astype(F32)).astype(BF16)
    rows, cols = attn.shape[1] // 2, out.shape[1] // 2
    for hop, ref in zip((0,) + HOPS, (here, ahead, behind, across)):
        place = lax.rem(y[0, 0] + hop, RING)
        odd, upper = lax.rem(place, 2), lax.div(place, 2)
        for block in range(rows // SPAN):
            start = (2 * block + odd) * SPAN
            ref[:, block * SPAN : (block + 1) * SPAN] = attn[:, pl.ds(pl.multiple_of(start, SPAN), SPAN)]
        ref[:, rows:] = out[:, pl.ds(pl.multiple_of(upper * cols, cols), cols)]


def d_image_call(cot, gate, adv, y, attn):
    rows, width = cot.shape
    vmem = pl.BlockSpec(memory_space=pltpu.VMEM)
    smem = pl.BlockSpec(memory_space=pltpu.SMEM)
    payload = jax.ShapeDtypeStruct((rows, attn.shape[1] // 2 + width // 2), BF16)
    return pl.pallas_call(
        d_image_kernel,
        in_specs=[vmem, vmem, smem, smem, vmem],
        out_specs=[vmem] * 5,
        out_shape=[jax.ShapeDtypeStruct((rows, width), BF16)] + [payload] * 4,
        compiler_params=params(48),
        cost_estimate=cost(2 * rows * width, 6 * rows * width),
    )(cot, gate, adv, y, attn)


def partial_kernel(c, m0, m1, m2, m3, keep, low, high):
    rows, half = keep.shape
    merged = (m0, m1, m2, m3)
    rhs = jnp.concatenate([ref[:, rows:] for ref in merged], axis=0)
    first = c[0, 0] == 0
    for start in range(0, rows, SPAN):
        lhs = jnp.concatenate([ref[:, start : start + SPAN] for ref in merged], axis=0)
        value = lax.dot_general(lhs, rhs, (((0,), (0,)), ((), ())), preferred_element_type=F32)
        left, right = value[:, :half], value[:, half:]
        keep[start : start + SPAN] = jnp.where(first, left, right).astype(BF16)
        out, skip = (low, 0) if start < rows // 2 else (high, rows // 2)
        out[start - skip : start - skip + SPAN] = jnp.where(first, right, left).astype(BF16)


def partial_call(c, merged, rows, cols):
    tokens = merged[0].shape[0]
    vmem = pl.BlockSpec(memory_space=pltpu.VMEM)
    return pl.pallas_call(
        partial_kernel,
        in_specs=[pl.BlockSpec(memory_space=pltpu.SMEM)] + [vmem] * len(merged),
        out_specs=[vmem] * 3,
        out_shape=[
            jax.ShapeDtypeStruct((rows, cols // 2), BF16),
            jax.ShapeDtypeStruct((rows // 2, cols // 2), BF16),
            jax.ShapeDtypeStruct((rows // 2, cols // 2), BF16),
        ],
        compiler_params=params(40),
        cost_estimate=cost(8 * tokens * rows * cols, 8 * tokens * (rows + cols) + 2 * rows * cols, SMALL),
    )(c, *merged)


def place_kernel(ring, keep, low, high, out, staged, sems):
    places, rows, _ = out.shape
    half = places // 2
    unit = rows // ring
    copies = []
    for part, got in enumerate((low, high)):
        for y in range(ring):
            for place in range(half):
                at = (y * half + place) * unit
                mine = keep[part * got.shape[0] + at : part * got.shape[0] + at + unit]
                value = mine.astype(F32) + got[at : at + unit].astype(F32)
                staged[part * half + place, y * unit : (y + 1) * unit] = value.astype(BF16)
        span = pl.ds(part * half, half)
        copies.append(pltpu.make_async_copy(staged.at[span], out.at[span], sems.at[part]))
        copies[-1].start()
    for copy in copies:
        copy.wait()


def place_call(keep, got, ring, places, rows):
    cols = keep.shape[1]
    shape = (len(got) * places, ring * rows, cols)
    vmem = pl.BlockSpec(memory_space=pltpu.VMEM)
    return pl.pallas_call(
        functools.partial(place_kernel, ring),
        in_specs=[vmem] * 3,
        out_specs=pl.BlockSpec(memory_space=pl.ANY),
        out_shape=jax.ShapeDtypeStruct(shape, BF16),
        scratch_shapes=[pltpu.VMEM(shape, BF16), pltpu.SemaphoreType.DMA((len(got),))],
        compiler_params=params(40),
        cost_estimate=cost(0, 6 * keep.size, SMALL),
    )(keep, *got)


def d_out_kernel(dimg, weight, cot_txt, adv, vt, vi, out):
    heads = out.shape[0]
    t = cot_txt.shape[0]
    total = lax.dot_general(dimg[...], weight[...], (((1,), (1,)), ((), ())), preferred_element_type=F32)
    total = total.astype(BF16)
    text = (adv[0, 0] * cot_txt[...].astype(F32)).astype(BF16)
    for h in range(heads):
        cols = slice(h * HEAD_SIZE, (h + 1) * HEAD_SIZE)
        out[h, :t, :HEAD_SIZE] = vt[:, cols]
        out[h, t:, :HEAD_SIZE] = vi[:, cols]
        out[h, :t, HEAD_SIZE:] = text[:, cols]
        out[h, t:, HEAD_SIZE:] = total[:, cols]


def d_out_call(dimg, weight, cot_txt, adv, txt, img, heads, step=8):
    rows, model = dimg.shape
    t = cot_txt.shape[0]
    width = step * HEAD_SIZE
    per = heads // step
    return pl.pallas_call(
        d_out_kernel,
        grid=(per,),
        in_specs=[
            pl.BlockSpec((rows, model), lambda g: (0, 0)),
            pl.BlockSpec((width, model), lambda g: (g, 0)),
            pl.BlockSpec((t, width), lambda g: (0, g)),
            pl.BlockSpec(memory_space=pltpu.SMEM),
            pl.BlockSpec((t, width), lambda g: (0, 2 * per + g)),
            pl.BlockSpec((rows, width), lambda g: (0, 2 * per + g)),
        ],
        out_specs=pl.BlockSpec((step, t + rows, 2 * HEAD_SIZE), lambda g: (g, 0, 0)),
        out_shape=jax.ShapeDtypeStruct((heads, t + rows, 2 * HEAD_SIZE), BF16),
        compiler_params=params(51),
        cost_estimate=cost(
            2 * rows * weight.size, 2 * (weight.size + dimg.size + 3 * (t + rows) * heads * HEAD_SIZE)
        ),
    )(dimg, weight, cot_txt, adv, txt, img)


def fold(array, combine):
    return combine(array.reshape(-1, 8, array.shape[1]), axis=0)


def exps_kernel(q, k, e_out, inv_out):
    chunks = [slice(at, at + CHUNK) for at in range(0, k.shape[0], CHUNK)]

    def scores(rows):
        return lax.dot_general(k[rows], q[...], (((1,), (1,)), ((), ())), preferred_element_type=F32)

    def fill(top):
        total = jnp.zeros((8, top.shape[1]), F32)
        top = top * (SCALE * LOG2E)
        for rows in chunks:
            low = jnp.exp2(scores(rows) * (SCALE * LOG2E) - top).astype(BF16)
            e_out[rows] = low
            total += fold(low.astype(F32), jnp.sum)
        total = jnp.sum(total, axis=0, keepdims=True)
        inv_out[...] = jnp.broadcast_to(1.0 / total, inv_out.shape)
        return total

    total = fill(jnp.max(scores(chunks[0]), axis=0, keepdims=True))

    @pl.when(jnp.logical_not(jnp.max(total) < SAFE))
    def _():
        top = None
        for rows in chunks:
            part = fold(scores(rows), jnp.max)
            top = part if top is None else jnp.maximum(top, part)
        fill(jnp.max(top, axis=0, keepdims=True))


def exps_call(qk):
    n = qk.shape[0]
    block = BLOCK
    return pl.pallas_call(
        exps_kernel,
        grid=(n // block,),
        in_specs=[
            pl.BlockSpec((block, HEAD_SIZE), lambda i: (i, 0)),
            pl.BlockSpec((n, HEAD_SIZE), lambda i: (0, 1)),
        ],
        out_specs=[
            pl.BlockSpec((n, block), lambda i: (0, i)),
            pl.BlockSpec((8, block), lambda i: (0, i)),
        ],
        out_shape=[
            jax.ShapeDtypeStruct((n, n), BF16),
            jax.ShapeDtypeStruct((8, n), F32),
        ],
        compiler_params=params(56),
        cost_estimate=cost(2 * n * n * HEAD_SIZE * 2, 2 * n * n, SMALL),
    )(qk, qk)


def grads_kernel(e, inv, q, k, v, d, out, dk, dv, prob_grads):
    step = pl.program_id(0)
    chunks = [slice(at, at + CHUNK) for at in range(0, k.shape[0], CHUNK)]

    @pl.when(step == 0)
    def _():
        dk[...] = jnp.zeros_like(dk)
        dv[...] = jnp.zeros_like(dv)

    inverse = jnp.transpose(jnp.broadcast_to(inv[:1], (HEAD_SIZE, BLOCK)))
    d_low = (d[...].astype(F32) * inverse).astype(BF16)
    centre = jnp.zeros((8, BLOCK), F32)
    for rows in chunks:
        probs = e[rows]
        part = lax.dot_general(v[rows], d_low, (((1,), (1,)), ((), ())), preferred_element_type=F32)
        prob_grads[rows] = part
        centre += fold(probs.astype(F32) * part, jnp.sum)
        dv[rows] += jnp.dot(probs, d_low, preferred_element_type=F32)
    centre = jnp.sum(centre, axis=0, keepdims=True) * inv[:1]
    dq = jnp.zeros((BLOCK, HEAD_SIZE), F32)
    for rows in chunks:
        score_grad = (e[rows].astype(F32) * (prob_grads[rows] - centre)).astype(BF16)
        dk[rows] += jnp.dot(score_grad, q[...], preferred_element_type=F32)
        dq += lax.dot_general(score_grad, k[rows], (((0,), (0,)), ((), ())), preferred_element_type=F32)
    out[pl.ds(pl.multiple_of(step * BLOCK, BLOCK), BLOCK), :HEAD_SIZE] = (dq * SCALE).astype(BF16)

    @pl.when(step == pl.num_programs(0) - 1)
    def _():
        out[:, HEAD_SIZE : 2 * HEAD_SIZE] = (dk[...] * SCALE).astype(BF16)
        out[:, 2 * HEAD_SIZE :] = dv[...].astype(BF16)


def grads_call(exps, inverse, qk, vd):
    n = qk.shape[0]
    block = lambda col: pl.BlockSpec((BLOCK, HEAD_SIZE), lambda i: (i, col))
    whole = lambda col: pl.BlockSpec((n, HEAD_SIZE), lambda i: (0, col))
    return pl.pallas_call(
        grads_kernel,
        grid=(n // BLOCK,),
        in_specs=[
            pl.BlockSpec((n, BLOCK), lambda i: (0, i)),
            pl.BlockSpec((8, BLOCK), lambda i: (0, i)),
            block(0),
            whole(1),
            whole(0),
            block(1),
        ],
        out_specs=pl.BlockSpec((n, 3 * HEAD_SIZE), lambda i: (0, 0)),
        out_shape=jax.ShapeDtypeStruct((n, 3 * HEAD_SIZE), BF16),
        scratch_shapes=[pltpu.VMEM((n, HEAD_SIZE), F32)] * 2 + [pltpu.VMEM((n, BLOCK), F32)],
        compiler_params=params(56),
        cost_estimate=cost(2 * n * n * HEAD_SIZE * 8, 2 * n * n, SMALL),
    )(exps, inverse, qk, qk, vd, vd)


def unpack_kernel(back, txt, img, txt_rows, img_rows, sems):
    heads, _, lanes = back.shape
    t = txt.shape[0]
    width = heads * HEAD_SIZE
    copies = []
    for slot in range(lanes // HEAD_SIZE):
        source = slice(slot * HEAD_SIZE, (slot + 1) * HEAD_SIZE)
        for h in range(heads):
            target = slice(slot * width + h * HEAD_SIZE, slot * width + (h + 1) * HEAD_SIZE)
            txt_rows[:, target] = back[h, :t, source]
            img_rows[:, target] = back[h, t:, source]
        whole = pl.ds(slot * width, width)
        for near, far in ((txt_rows, txt), (img_rows, img)):
            copy = pltpu.make_async_copy(near.at[:, whole], far.at[:, whole], sems.at[len(copies)])
            copy.start()
            copies.append(copy)
    for copy in copies:
        copy.wait()


def unpack_call(back, t):
    heads, tokens, lanes = back.shape
    shapes = [(t, heads * lanes), (tokens - t, heads * lanes)]
    return pl.pallas_call(
        unpack_kernel,
        in_specs=[pl.BlockSpec(memory_space=pltpu.VMEM)],
        out_specs=[pl.BlockSpec(memory_space=pl.ANY)] * 2,
        out_shape=[jax.ShapeDtypeStruct(shape, BF16) for shape in shapes],
        scratch_shapes=[pltpu.VMEM(shape, BF16) for shape in shapes]
        + [pltpu.SemaphoreType.DMA((2 * lanes // HEAD_SIZE,))],
        compiler_params=params(24),
        cost_estimate=cost(0, 2 * back.size, SMALL),
    )(back)


def per_device(qkv_txt, qkv_img, attn_img, cot_txt, cot_img, gate, advantage, proj_weight):
    txt, img = qkv_txt[0], qkv_img[0]
    tokens = txt.shape[0] + img.shape[0]
    width = attn_img.shape[2]
    heads = width // HEAD_SIZE
    model = cot_img.shape[2]
    adv = advantage[:, None]
    index = lambda axes: lax.axis_index(axes).astype(jnp.int32).reshape(1, 1)
    y, core = index("y"), index("c")

    def shift(arrays, axes):
        perms = [[(i, (i + hop) % RING) for i in range(RING)] for hop in HOPS]
        return [lax.ppermute(array, axes, perm) for array, perm in zip(arrays, perms)]

    def swap(array):
        return lax.ppermute(array, "c", [(0, 1), (1, 0)])

    attn = attn_img[0]
    packed = pack_heads(txt, img, 0, 2, heads)
    qk = exchange(packed, SEQ)
    cot, attn, packed = lax.optimization_barrier((cot_img[0], attn, packed))
    d_image, here, *merged = d_image_call(cot, gate, adv, y, attn)
    merged = [here, *shift(merged, "y")]
    vd = d_out_call(d_image, proj_weight, cot_txt[0], adv, txt, img, heads)
    vd, qk = lax.optimization_barrier((vd, qk))
    vd = exchange(vd, SEQ)

    n = heads * tokens
    qk = qk.reshape(n, 2 * HEAD_SIZE)
    exps, inverse = exps_call(qk)
    merged, inverse = lax.optimization_barrier((merged, inverse))
    keep, low, high = partial_call(core, merged, width // 2, model // 2)
    low, high = swap(low), swap(high)

    devices = lax.axis_size(ALL)
    rows = width // devices
    cols = keep.shape[1]
    product = place_call(keep, [low, high], RING // 2, lax.axis_size(PLANE) // 2, 2 * rows)
    product = exchange(product, PLANE)

    vd = vd.reshape(n, 2 * HEAD_SIZE)
    grads = grads_call(exps, inverse, qk, vd).reshape(heads, tokens, 3 * HEAD_SIZE)
    grads, product = lax.optimization_barrier((grads, product))
    back = exchange(grads, SEQ)

    total = jnp.sum(product.astype(F32), axis=0) * (1.0 / (img.shape[0] * devices))
    total = total.reshape(2, 2, rows, cols)
    c, upper = core[0, 0], y[0, 0] // 2

    def joined(first, own, other):
        return jnp.where(first, jnp.concatenate([own, other], -1), jnp.concatenate([other, own], -1))

    own = lax.dynamic_index_in_dim(total, c, 1, keepdims=False)
    other = swap(lax.dynamic_index_in_dim(total, 1 - c, 1, keepdims=False))
    wide = joined(c == 0, own, other)
    own = lax.dynamic_index_in_dim(wide, upper, 0, keepdims=False)
    other = lax.dynamic_index_in_dim(wide, 1 - upper, 0, keepdims=False)
    other = lax.ppermute(other, "y", [(i, (i + 2) % RING) for i in range(RING)])
    grad_proj = joined(upper == 0, own, other)
    back, grad_proj = lax.optimization_barrier((back, grad_proj))

    dqkv_txt, dqkv_img = unpack_call(back, txt.shape[0])
    return (dqkv_txt[None], dqkv_img[None], grad_proj)


def solution(mesh):
    fine = Mesh(mesh.devices.reshape(2, 4, 2, 4, 2), ALL)
    dp = ("zh", "y")
    tokens = P(dp, SEQ, None)
    return jax.shard_map(
        per_device,
        mesh=fine,
        in_specs=(tokens, tokens, tokens, tokens, tokens, P(dp, None), P(dp), P()),
        out_specs=(tokens, tokens, P(dp + SEQ, None)),
        check_vma=False,
    )
```

```python
import functools

import jax
import jax.numpy as jnp
from jax import lax
from jax.experimental import pallas as pl
from jax.experimental.pallas import tpu as pltpu
from jax.sharding import Mesh, PartitionSpec as P

HEAD_SIZE = 128
SCALE = HEAD_SIZE ** (-0.5)
LOG2E = 1.4426950408889634
BLOCK = 512
CHUNK = 256
WIDE = 1280
SMALL = 1000
SAFE = 2.0**40
SEQ = ("zl", "x", "c")
ALL = ("zh", "y", "zl", "x", "c")
PLANE = ("zh", "zl", "x")
RING = 4
HOPS = (1, RING - 1, 2)
SPAN = 256
BF16 = jnp.bfloat16
F32 = jnp.float32


def exchange(array, axes):
    return lax.all_to_all(array, axes, split_axis=0, concat_axis=0, tiled=True)


def params(mib):
    return pltpu.CompilerParams(vmem_limit_bytes=mib << 20)


def cost(flops, nbytes, part=1):
    return pl.CostEstimate(flops=flops // part, bytes_accessed=nbytes // part, transcendentals=0)


def pack_kernel(slots, *refs):
    out = refs[-1]
    txt, img = refs[:slots], refs[slots : 2 * slots]
    heads = out.shape[0]
    t = txt[0].shape[0]
    for j in range(slots):
        lanes = slice(j * HEAD_SIZE, (j + 1) * HEAD_SIZE)
        for h in range(heads):
            cols = slice(h * HEAD_SIZE, (h + 1) * HEAD_SIZE)
            out[h, :t, lanes] = txt[j][:, cols]
            out[h, t:, lanes] = img[j][:, cols]


def pack_heads(txt, img, first, slots, heads, step=8):
    t, i = txt.shape[0], img.shape[0]
    per = heads // step

    def spec(rows, j):
        return pl.BlockSpec((rows, step * HEAD_SIZE), lambda g: (0, (first + j) * per + g))

    nbytes = 2 * (t + i) * slots * heads * HEAD_SIZE * 2
    return pl.pallas_call(
        functools.partial(pack_kernel, slots),
        grid=(per,),
        in_specs=[spec(t, j) for j in range(slots)] + [spec(i, j) for j in range(slots)],
        out_specs=pl.BlockSpec((step, t + i, slots * HEAD_SIZE), lambda g: (g, 0, 0)),
        out_shape=jax.ShapeDtypeStruct((heads, t + i, slots * HEAD_SIZE), BF16),
        compiler_params=params(56),
        cost_estimate=cost(0, nbytes),
    )(*([txt] * slots), *([img] * slots))


def d_image_kernel(cot, gate, adv, y, attn, out, here, ahead, behind, across):
    weighted = adv[0, 0] * gate[...]
    out[...] = (weighted * cot[...].astype(F32)).astype(BF16)
    rows, cols = attn.shape[1] // 2, out.shape[1] // 2
    for hop, ref in zip((0,) + HOPS, (here, ahead, behind, across)):
        place = lax.rem(y[0, 0] + hop, RING)
        odd, upper = lax.rem(place, 2), lax.div(place, 2)
        for block in range(rows // SPAN):
            start = (2 * block + odd) * SPAN
            ref[:, block * SPAN : (block + 1) * SPAN] = attn[:, pl.ds(pl.multiple_of(start, SPAN), SPAN)]
        ref[:, rows:] = out[:, pl.ds(pl.multiple_of(upper * cols, cols), cols)]


def d_image_call(cot, gate, adv, y, attn):
    rows, width = cot.shape
    vmem = pl.BlockSpec(memory_space=pltpu.VMEM)
    smem = pl.BlockSpec(memory_space=pltpu.SMEM)
    payload = jax.ShapeDtypeStruct((rows, attn.shape[1] // 2 + width // 2), BF16)
    return pl.pallas_call(
        d_image_kernel,
        in_specs=[vmem, vmem, smem, smem, vmem],
        out_specs=[vmem] * 5,
        out_shape=[jax.ShapeDtypeStruct((rows, width), BF16)] + [payload] * 4,
        compiler_params=params(48),
        cost_estimate=cost(2 * rows * width, 6 * rows * width),
    )(cot, gate, adv, y, attn)


def partial_kernel(c, m0, m1, m2, m3, keep, low, high):
    rows, half = keep.shape
    merged = (m0, m1, m2, m3)
    rhs = jnp.concatenate([ref[:, rows:] for ref in merged], axis=0)
    first = c[0, 0] == 0
    for start in range(0, rows, SPAN):
        lhs = jnp.concatenate([ref[:, start : start + SPAN] for ref in merged], axis=0)
        value = lax.dot_general(lhs, rhs, (((0,), (0,)), ((), ())), preferred_element_type=F32)
        left, right = value[:, :half], value[:, half:]
        keep[start : start + SPAN] = jnp.where(first, left, right).astype(BF16)
        out, skip = (low, 0) if start < rows // 2 else (high, rows // 2)
        out[start - skip : start - skip + SPAN] = jnp.where(first, right, left).astype(BF16)


def partial_call(c, merged, rows, cols):
    tokens = merged[0].shape[0]
    vmem = pl.BlockSpec(memory_space=pltpu.VMEM)
    return pl.pallas_call(
        partial_kernel,
        in_specs=[pl.BlockSpec(memory_space=pltpu.SMEM)] + [vmem] * len(merged),
        out_specs=[vmem] * 3,
        out_shape=[
            jax.ShapeDtypeStruct((rows, cols // 2), BF16),
            jax.ShapeDtypeStruct((rows // 2, cols // 2), BF16),
            jax.ShapeDtypeStruct((rows // 2, cols // 2), BF16),
        ],
        compiler_params=params(40),
        cost_estimate=cost(8 * tokens * rows * cols, 8 * tokens * (rows + cols) + 2 * rows * cols, SMALL),
    )(c, *merged)


def place_kernel(ring, keep, low, high, out, staged, sems):
    places, rows, _ = out.shape
    half = places // 2
    unit = rows // ring
    copies = []
    for part, got in enumerate((low, high)):
        for y in range(ring):
            for place in range(half):
                at = (y * half + place) * unit
                mine = keep[part * got.shape[0] + at : part * got.shape[0] + at + unit]
                value = mine.astype(F32) + got[at : at + unit].astype(F32)
                staged[part * half + place, y * unit : (y + 1) * unit] = value.astype(BF16)
        span = pl.ds(part * half, half)
        copies.append(pltpu.make_async_copy(staged.at[span], out.at[span], sems.at[part]))
        copies[-1].start()
    for copy in copies:
        copy.wait()


def place_call(keep, got, ring, places, rows):
    cols = keep.shape[1]
    shape = (len(got) * places, ring * rows, cols)
    vmem = pl.BlockSpec(memory_space=pltpu.VMEM)
    return pl.pallas_call(
        functools.partial(place_kernel, ring),
        in_specs=[vmem] * 3,
        out_specs=pl.BlockSpec(memory_space=pl.ANY),
        out_shape=jax.ShapeDtypeStruct(shape, BF16),
        scratch_shapes=[pltpu.VMEM(shape, BF16), pltpu.SemaphoreType.DMA((len(got),))],
        compiler_params=params(40),
        cost_estimate=cost(0, 6 * keep.size, SMALL),
    )(keep, *got)


def d_out_kernel(dimg, weight, cot_txt, adv, vt, vi, out):
    heads = out.shape[0]
    t = cot_txt.shape[0]
    total = lax.dot_general(dimg[...], weight[...], (((1,), (1,)), ((), ())), preferred_element_type=F32)
    total = total.astype(BF16)
    text = (adv[0, 0] * cot_txt[...].astype(F32)).astype(BF16)
    for h in range(heads):
        cols = slice(h * HEAD_SIZE, (h + 1) * HEAD_SIZE)
        out[h, :t, :HEAD_SIZE] = vt[:, cols]
        out[h, t:, :HEAD_SIZE] = vi[:, cols]
        out[h, :t, HEAD_SIZE:] = text[:, cols]
        out[h, t:, HEAD_SIZE:] = total[:, cols]


def d_out_call(dimg, weight, cot_txt, adv, txt, img, heads, step=8):
    rows, model = dimg.shape
    t = cot_txt.shape[0]
    width = step * HEAD_SIZE
    per = heads // step
    return pl.pallas_call(
        d_out_kernel,
        grid=(per,),
        in_specs=[
            pl.BlockSpec((rows, model), lambda g: (0, 0)),
            pl.BlockSpec((width, model), lambda g: (g, 0)),
            pl.BlockSpec((t, width), lambda g: (0, g)),
            pl.BlockSpec(memory_space=pltpu.SMEM),
            pl.BlockSpec((t, width), lambda g: (0, 2 * per + g)),
            pl.BlockSpec((rows, width), lambda g: (0, 2 * per + g)),
        ],
        out_specs=pl.BlockSpec((step, t + rows, 2 * HEAD_SIZE), lambda g: (g, 0, 0)),
        out_shape=jax.ShapeDtypeStruct((heads, t + rows, 2 * HEAD_SIZE), BF16),
        compiler_params=params(51),
        cost_estimate=cost(
            2 * rows * weight.size, 2 * (weight.size + dimg.size + 3 * (t + rows) * heads * HEAD_SIZE)
        ),
    )(dimg, weight, cot_txt, adv, txt, img)


def fold(array, combine):
    return combine(array.reshape(-1, 8, array.shape[1]), axis=0)


def block_copies(array, buffer, sems, step, back):
    slot = lax.rem(step, 2)
    columns = pl.ds(pl.multiple_of(step * WIDE, WIDE), WIDE)
    copies = []
    for chunk in range(array.shape[0] // CHUNK):
        rows = pl.ds(chunk * CHUNK, CHUNK)
        far, near = array.at[rows, columns], buffer.at[slot, rows]
        source, target = (near, far) if back else (far, near)
        copies.append(pltpu.make_async_copy(source, target, sems.at[slot, chunk]))
    return copies


def exps_kernel(q, k, e_out, inv_out, buffer, sems):
    step, last = pl.program_id(0), pl.num_programs(0) - 1
    slot = lax.rem(step, 2)
    chunks = [slice(at, at + CHUNK) for at in range(0, k.shape[0], CHUNK)]
    copies = block_copies(e_out, buffer, sems, step, True)

    @pl.when(step >= 2)
    def _():
        for copy in block_copies(e_out, buffer, sems, step - 2, True):
            copy.wait()

    def scores(rows):
        return lax.dot_general(k[rows], q[...], (((1,), (1,)), ((), ())), preferred_element_type=F32)

    def fill(top):
        total = jnp.zeros((8, top.shape[1]), F32)
        top = top * (SCALE * LOG2E)
        for rows, copy in zip(chunks, copies):
            low = jnp.exp2(scores(rows) * (SCALE * LOG2E) - top).astype(BF16)
            buffer[slot, rows] = low
            copy.start()
            total += fold(low.astype(F32), jnp.sum)
        total = jnp.sum(total, axis=0, keepdims=True)
        inv_out[...] = jnp.broadcast_to(1.0 / total, inv_out.shape)
        return total

    total = fill(jnp.max(scores(chunks[0]), axis=0, keepdims=True))

    @pl.when(jnp.logical_not(jnp.max(total) < SAFE))
    def _():
        top = None
        for rows, copy in zip(chunks, copies):
            copy.wait()
            part = fold(scores(rows), jnp.max)
            top = part if top is None else jnp.maximum(top, part)
        fill(jnp.max(top, axis=0, keepdims=True))

    @pl.when(step == last)
    def _():
        for copy in block_copies(e_out, buffer, sems, step - 1, True) + copies:
            copy.wait()


def exps_call(qk):
    n = qk.shape[0]
    return pl.pallas_call(
        exps_kernel,
        grid=(n // WIDE,),
        in_specs=[
            pl.BlockSpec((WIDE, HEAD_SIZE), lambda i: (i, 0)),
            pl.BlockSpec((n, HEAD_SIZE), lambda i: (0, 1)),
        ],
        out_specs=[
            pl.BlockSpec(memory_space=pl.ANY),
            pl.BlockSpec((8, WIDE), lambda i: (0, i)),
        ],
        out_shape=[
            jax.ShapeDtypeStruct((n, n), BF16),
            jax.ShapeDtypeStruct((8, n), F32),
        ],
        scratch_shapes=[pltpu.VMEM((2, n, WIDE), BF16), pltpu.SemaphoreType.DMA((2, n // CHUNK))],
        compiler_params=params(56),
        cost_estimate=cost(2 * n * n * HEAD_SIZE * 2, 2 * n * n, SMALL),
    )(qk, qk)


def grads_kernel(e, inv, q, k, v, d, out, dk, dv, prob_grads):
    step = pl.program_id(0)
    chunks = [slice(at, at + CHUNK) for at in range(0, k.shape[0], CHUNK)]

    @pl.when(step == 0)
    def _():
        dk[...] = jnp.zeros_like(dk)
        dv[...] = jnp.zeros_like(dv)

    inverse = jnp.transpose(jnp.broadcast_to(inv[:1], (HEAD_SIZE, BLOCK)))
    d_low = (d[...].astype(F32) * inverse).astype(BF16)
    centre = jnp.zeros((8, BLOCK), F32)
    for rows in chunks:
        probs = e[rows]
        part = lax.dot_general(v[rows], d_low, (((1,), (1,)), ((), ())), preferred_element_type=F32)
        prob_grads[rows] = part
        centre += fold(probs.astype(F32) * part, jnp.sum)
        dv[rows] += jnp.dot(probs, d_low, preferred_element_type=F32)
    centre = jnp.sum(centre, axis=0, keepdims=True) * inv[:1]
    dq = jnp.zeros((BLOCK, HEAD_SIZE), F32)
    for rows in chunks:
        score_grad = (e[rows].astype(F32) * (prob_grads[rows] - centre)).astype(BF16)
        dk[rows] += jnp.dot(score_grad, q[...], preferred_element_type=F32)
        dq += lax.dot_general(score_grad, k[rows], (((0,), (0,)), ((), ())), preferred_element_type=F32)
    out[pl.ds(pl.multiple_of(step * BLOCK, BLOCK), BLOCK), :HEAD_SIZE] = (dq * SCALE).astype(BF16)

    @pl.when(step == pl.num_programs(0) - 1)
    def _():
        out[:, HEAD_SIZE : 2 * HEAD_SIZE] = (dk[...] * SCALE).astype(BF16)
        out[:, 2 * HEAD_SIZE :] = dv[...].astype(BF16)


def grads_call(exps, inverse, qk, vd):
    n = qk.shape[0]
    block = lambda col: pl.BlockSpec((BLOCK, HEAD_SIZE), lambda i: (i, col))
    whole = lambda col: pl.BlockSpec((n, HEAD_SIZE), lambda i: (0, col))
    return pl.pallas_call(
        grads_kernel,
        grid=(n // BLOCK,),
        in_specs=[
            pl.BlockSpec((n, BLOCK), lambda i: (0, i)),
            pl.BlockSpec((8, BLOCK), lambda i: (0, i)),
            block(0),
            whole(1),
            whole(0),
            block(1),
        ],
        out_specs=pl.BlockSpec((n, 3 * HEAD_SIZE), lambda i: (0, 0)),
        out_shape=jax.ShapeDtypeStruct((n, 3 * HEAD_SIZE), BF16),
        scratch_shapes=[pltpu.VMEM((n, HEAD_SIZE), F32)] * 2 + [pltpu.VMEM((n, BLOCK), F32)],
        compiler_params=params(56),
        cost_estimate=cost(2 * n * n * HEAD_SIZE * 8, 2 * n * n, SMALL),
    )(exps, inverse, qk, qk, vd, vd)


def unpack_kernel(back, txt, img, txt_rows, img_rows, sems):
    heads, _, lanes = back.shape
    t = txt.shape[0]
    width = heads * HEAD_SIZE
    copies = []
    for slot in range(lanes // HEAD_SIZE):
        source = slice(slot * HEAD_SIZE, (slot + 1) * HEAD_SIZE)
        for h in range(heads):
            target = slice(slot * width + h * HEAD_SIZE, slot * width + (h + 1) * HEAD_SIZE)
            txt_rows[:, target] = back[h, :t, source]
            img_rows[:, target] = back[h, t:, source]
        whole = pl.ds(slot * width, width)
        for near, far in ((txt_rows, txt), (img_rows, img)):
            copy = pltpu.make_async_copy(near.at[:, whole], far.at[:, whole], sems.at[len(copies)])
            copy.start()
            copies.append(copy)
    for copy in copies:
        copy.wait()


def unpack_call(back, t):
    heads, tokens, lanes = back.shape
    shapes = [(t, heads * lanes), (tokens - t, heads * lanes)]
    return pl.pallas_call(
        unpack_kernel,
        in_specs=[pl.BlockSpec(memory_space=pltpu.VMEM)],
        out_specs=[pl.BlockSpec(memory_space=pl.ANY)] * 2,
        out_shape=[jax.ShapeDtypeStruct(shape, BF16) for shape in shapes],
        scratch_shapes=[pltpu.VMEM(shape, BF16) for shape in shapes]
        + [pltpu.SemaphoreType.DMA((2 * lanes // HEAD_SIZE,))],
        compiler_params=params(24),
        cost_estimate=cost(0, 2 * back.size, SMALL),
    )(back)


def per_device(qkv_txt, qkv_img, attn_img, cot_txt, cot_img, gate, advantage, proj_weight):
    txt, img = qkv_txt[0], qkv_img[0]
    tokens = txt.shape[0] + img.shape[0]
    width = attn_img.shape[2]
    heads = width // HEAD_SIZE
    model = cot_img.shape[2]
    adv = advantage[:, None]
    index = lambda axes: lax.axis_index(axes).astype(jnp.int32).reshape(1, 1)
    y, core = index("y"), index("c")

    def shift(arrays, axes):
        perms = [[(i, (i + hop) % RING) for i in range(RING)] for hop in HOPS]
        return [lax.ppermute(array, axes, perm) for array, perm in zip(arrays, perms)]

    def swap(array):
        return lax.ppermute(array, "c", [(0, 1), (1, 0)])

    attn = attn_img[0]
    packed = pack_heads(txt, img, 0, 2, heads)
    qk = exchange(packed, SEQ)
    cot, attn, packed = lax.optimization_barrier((cot_img[0], attn, packed))
    d_image, here, *merged = d_image_call(cot, gate, adv, y, attn)
    merged = [here, *shift(merged, "y")]
    vd = d_out_call(d_image, proj_weight, cot_txt[0], adv, txt, img, heads)
    vd, qk = lax.optimization_barrier((vd, qk))
    vd = exchange(vd, SEQ)

    n = heads * tokens
    qk = qk.reshape(n, 2 * HEAD_SIZE)
    exps, inverse = exps_call(qk)
    merged, inverse = lax.optimization_barrier((merged, inverse))
    keep, low, high = partial_call(core, merged, width // 2, model // 2)
    low, high = swap(low), swap(high)

    devices = lax.axis_size(ALL)
    rows = width // devices
    cols = keep.shape[1]
    product = place_call(keep, [low, high], RING // 2, lax.axis_size(PLANE) // 2, 2 * rows)
    product = exchange(product, PLANE)

    vd = vd.reshape(n, 2 * HEAD_SIZE)
    grads = grads_call(exps, inverse, qk, vd).reshape(heads, tokens, 3 * HEAD_SIZE)
    grads, product = lax.optimization_barrier((grads, product))
    back = exchange(grads, SEQ)

    total = jnp.sum(product.astype(F32), axis=0) * (1.0 / (img.shape[0] * devices))
    total = total.reshape(2, 2, rows, cols)
    c, upper = core[0, 0], y[0, 0] // 2

    def joined(first, own, other):
        return jnp.where(first, jnp.concatenate([own, other], -1), jnp.concatenate([other, own], -1))

    own = lax.dynamic_index_in_dim(total, c, 1, keepdims=False)
    other = swap(lax.dynamic_index_in_dim(total, 1 - c, 1, keepdims=False))
    wide = joined(c == 0, own, other)
    own = lax.dynamic_index_in_dim(wide, upper, 0, keepdims=False)
    other = lax.dynamic_index_in_dim(wide, 1 - upper, 0, keepdims=False)
    other = lax.ppermute(other, "y", [(i, (i + 2) % RING) for i in range(RING)])
    grad_proj = joined(upper == 0, own, other)
    back, grad_proj = lax.optimization_barrier((back, grad_proj))

    dqkv_txt, dqkv_img = unpack_call(back, txt.shape[0])
    return (dqkv_txt[None], dqkv_img[None], grad_proj)


def solution(mesh):
    fine = Mesh(mesh.devices.reshape(2, 4, 2, 4, 2), ALL)
    dp = ("zh", "y")
    tokens = P(dp, SEQ, None)
    return jax.shard_map(
        per_device,
        mesh=fine,
        in_specs=(tokens, tokens, tokens, tokens, tokens, P(dp, None), P(dp), P()),
        out_specs=(tokens, tokens, P(dp + SEQ, None)),
        check_vma=False,
    )
```
